512 devices in a mesh: member: 8 (over x, z_hi), node: 64 (over z_lo, y, core).
Axes of the slice: x: 4, y: 8, z: 8 (z_hi: 2, z_lo: 4; z = z_hi * 4 + z_lo), core: 2. Of those that a mesh axis runs over, the one named last changes fastest.
Arguments:
- latent: bfloat16 [16, 16384, 512], P('member', 'node'), may hold values from -6 to 6
- noise_draw: float32 [16, 32], P('member'), may hold values from -4 to 4
- mesh_links: int32 [6, 16384], P(None, 'node'), may hold values from 0 to 16383, as said below
- w_cond: float32 [2, 32, 512], replicated, may hold values from -0.3 to 0.3
- w_in: bfloat16 [2, 1024, 512], replicated, may hold values from -0.1875 to 0.1875
- w_out: bfloat16 [2, 512, 512], replicated, may hold values from -0.25 to 0.25
- dec_gain: float32 [512], replicated, may hold values from 0.5 to 1.5
- w_dec: bfloat16 [83, 512], replicated, may hold values from -2 to 2
- target_vertex_map: int32 [65536], P('node'), may hold values from 0 to 16383, as said below
- prior_field: bfloat16 [83, 65536], P(None, 'node'), may hold values from -6 to 6
- target: bfloat16 [83, 65536], P(None, 'node'), may hold values from -6 to 6
- location_loss_factor: float32 [65536], P('node'), may hold values from 8 to 24
Outputs:
- prediction_sensitivity: bfloat16 [16, 83, 65536], P('member', None, 'node')
- vertex_attribute_sensitivity: bfloat16 [16, 16384, 512], P('member', 'node')
The draws below stay inside these ranges and needn't reach their ends.
Inputs may be any that keep to these rules, and one draw needn't show every extreme that they name: mesh_links[k, n] = (n + s) mod 16384 with 1 <= |s| <= 96: every neighbour of a node lies within 96 positions of it along the node order, counted around the end. target_vertex_map[g] // 256 == g // 1024.
All inputs are finite; a program needn't handle non-finite values.
Results may differ from the reference program's by a relative error of at most 0.007.
Values may be sent and summed in bfloat16 or wider, within the bound.
No kernel may reach another device: no remote copies, remote signals or barrier semaphores. Data moves between devices by JAX's collectives and lax.ppermute only.
A program may use at most 64 MiB of HBM per device.

```python
import math
import jax
import jax.numpy as jnp
from jax import lax

LAT = 512
CH = 83
NOISE = 32
LAYERS = 2
LINKS = 6
WIN = 96
NODE_DEV = 256
GRID_DEV = 1024
MEMBERS = 16
NODES = 16384
GRID = 65536


def draw_mesh_links(key, part):
    magnitude = jax.random.randint(jax.random.fold_in(key, 11), (LINKS, NODES), 1, WIN + 1)
    direction = jax.random.randint(jax.random.fold_in(key, 12), (LINKS, NODES), 0, 2) * 2 - 1
    positions = jnp.arange(NODES, dtype=jnp.int32)[None, :]
    return jnp.mod(positions + magnitude * direction, NODES).astype(jnp.int32)


def draw_target_vertex_map(key, part):
    local_node = jax.random.randint(jax.random.fold_in(key, 21), (GRID,), 0, NODE_DEV)
    shard_index = jnp.arange(GRID, dtype=jnp.int32) // GRID_DEV
    return (shard_index * NODE_DEV + local_node).astype(jnp.int32)


def draw_w_dec(key, part):
    levels = jax.random.uniform(jax.random.fold_in(key, 31), (CH, 1), jnp.float32, 0.0, jnp.log(32.0))
    row_scale = jnp.exp(levels)
    row_scale = row_scale / jnp.sqrt(jnp.mean(row_scale * row_scale))
    entries = jax.random.normal(jax.random.fold_in(key, 33), (CH, LAT), jnp.float32) * row_scale / jnp.sqrt(jnp.float32(LAT))
    return jnp.clip(entries, -2.0, 2.0).astype(jnp.bfloat16)


def shard_levels(key, dims, shards, low, high):
    factor_of, own = 1.0, jax.random.fold_in(key, 6)
    for position, parts in shards:
        heights = jnp.exp(jax.random.uniform(jax.random.fold_in(own, position), (parts,), jnp.float32, low / len(shards), high / len(shards)))
        factor_of = factor_of * jnp.repeat(heights, dims[position] // parts).reshape([-1 if axis == position else 1 for axis in range(len(dims))])
    return factor_of


def normal_values(stream_key, dims, deviation, reach, pieces=(), kind=jnp.bfloat16):
    gain = shard_levels(stream_key, dims, pieces, -0.22, 0.18) if pieces else 1.0
    array = jax.random.normal(stream_key, dims, jnp.float32) * deviation * gain
    return jnp.minimum(jnp.maximum(array, -reach), reach).astype(kind)


def setup_inputs(seed: int = 0) -> dict:
    seeds = jax.random.split(jax.random.key(seed), 13)
    latent = normal_values(seeds[0], (MEMBERS, NODES, LAT), 1.0, 6.0, ((0, 8), (1, 64)))
    noise_draw = normal_values(seeds[1], (MEMBERS, NOISE), 1.0, 4.0, ((0, 8),), jnp.float32)
    mesh_links = draw_mesh_links(jax.random.fold_in(seeds[12], 71), 0)
    w_cond = normal_values(seeds[3], (LAYERS, NOISE, LAT), 0.05, 0.3, (), jnp.float32)
    w_in = normal_values(seeds[4], (LAYERS, 2 * LAT, LAT), (2 * LAT) ** -0.5, 0.1875)
    w_out = normal_values(seeds[5], (LAYERS, LAT, LAT), LAT ** -0.5, 0.25)
    dec_gain = jnp.clip(1.0 + 0.1 * jax.random.normal(seeds[6], (LAT,), jnp.float32), 0.5, 1.5)
    w_dec = draw_w_dec(jax.random.fold_in(seeds[12], 71), 0)
    target_vertex_map = draw_target_vertex_map(jax.random.fold_in(seeds[12], 71), 0)
    prior_field = normal_values(seeds[9], (CH, GRID), 1.0, 6.0, ((1, 64),))
    target = normal_values(seeds[10], (CH, GRID), 1.0, 6.0, ((1, 64),))
    location_loss_factor = jnp.clip(jnp.exp(math.log(24.0) - 1.0986123 * jax.random.uniform(seeds[11], (GRID,), jnp.float32) ** shard_levels(seeds[11], (GRID,), ((0, 64),), -0.2, 0.2)), 8.0, 24.0)
    return dict(latent=latent, noise_draw=noise_draw, mesh_links=mesh_links, w_cond=w_cond, w_in=w_in, w_out=w_out, dec_gain=dec_gain, w_dec=w_dec, target_vertex_map=target_vertex_map, prior_field=prior_field, target=target, location_loss_factor=location_loss_factor)


NORM_EPS = 1e-06
DIST_EPS = 1e-06

def apply_layer_norm(values, scaling):
    inverse = lax.rsqrt(lax.optimization_barrier(jnp.mean(values * values, axis=-1, keepdims=True)) + NORM_EPS)
    return (values * inverse * scaling).astype(jnp.bfloat16)

def member_features(latent_row, noise_row, mesh_links, w_cond, w_in, w_out, dec_gain):
    processor_state = latent_row.astype(jnp.float32)
    for current_layer_index in range(LAYERS):
        scaling = 1.0 + jnp.dot(noise_row, w_cond[current_layer_index], precision=lax.Precision.HIGHEST)
        normalized_rows = apply_layer_norm(processor_state, scaling)
        summed = jnp.zeros(processor_state.shape, jnp.float32)
        for slot_index in range(LINKS):
            summed = summed + jnp.take(normalized_rows, mesh_links[slot_index], axis=0).astype(jnp.float32)
        neighbours = (summed / LINKS).astype(jnp.bfloat16)
        joined = jnp.concatenate([normalized_rows, neighbours], axis=1)
        preact = jnp.dot(joined, w_in[current_layer_index], preferred_element_type=jnp.float32)
        activated = jax.nn.silu(preact).astype(jnp.bfloat16)
        processor_state = processor_state + jnp.dot(activated, w_out[current_layer_index], preferred_element_type=jnp.float32)
    return apply_layer_norm(processor_state, dec_gain)

def reference(latent, noise_draw, mesh_links, w_cond, w_in, w_out, dec_gain, w_dec, target_vertex_map, prior_field, target, location_loss_factor):

    def per_member(operands):
        latent_row, noise_row = operands
        features = member_features(latent_row, noise_row, mesh_links, w_cond, w_in, w_out, dec_gain)
        return jnp.dot(w_dec, features.T, preferred_element_type=jnp.float32)
    readout_result = lax.map(per_member, (latent, noise_draw))
    ensemble_prediction = (prior_field.astype(jnp.float32)[None] + jnp.take(readout_result, target_vertex_map, axis=2)).astype(jnp.bfloat16)
    ensemble_size = ensemble_prediction.astype(jnp.float32)
    truth_all = target.astype(jnp.float32)

    def add_pull(carried, other_member):
        offset = ensemble_size - other_member[None]
        spread = jnp.sqrt(lax.optimization_barrier(jnp.sum(offset * offset, axis=1, keepdims=True)) + DIST_EPS)
        return (carried + offset / spread, None)
    pull_sums = lax.scan(add_pull, jnp.zeros_like(ensemble_size), ensemble_size)[0]
    missed = ensemble_size - truth_all[None]
    reached = jnp.sqrt(lax.optimization_barrier(jnp.sum(missed * missed, axis=1, keepdims=True)) + DIST_EPS)
    ensemble = MEMBERS
    skill_measures = missed / (ensemble * reached) - pull_sums / (ensemble * (ensemble - 1))
    prediction_sensitivity = (location_loss_factor[None, None, :] * skill_measures).astype(jnp.bfloat16)

    def per_vertex_quantities(grad_row):
        return jax.ops.segment_sum(grad_row.astype(jnp.float32).T, target_vertex_map, num_segments=NODES)
    vertex_sensitivity = lax.map(per_vertex_quantities, prediction_sensitivity)
    vertex_attribute_sensitivity = jnp.einsum('mnc,cl->mnl', vertex_sensitivity, w_dec.astype(jnp.float32), precision=lax.Precision.HIGHEST).astype(jnp.bfloat16)
    return (prediction_sensitivity, vertex_attribute_sensitivity)
```

```python
import functools

import jax
import jax.numpy as jnp
from jax import lax
from jax.experimental import pallas as pl
from jax.experimental.pallas import tpu as pltpu
from jax.sharding import PartitionSpec as P

WIN = 96
NORM_EPS = 1e-06
DIST_EPS = 1e-06

BF = jnp.bfloat16
F32 = jnp.float32
VMEM = pl.BlockSpec(memory_space=pltpu.VMEM)
SMEM = pl.BlockSpec(memory_space=pltpu.SMEM)
PARAMS = pltpu.CompilerParams(vmem_limit_bytes=40 * 2**20)


def dot(lhs, rhs):
    return jnp.dot(lhs, rhs, preferred_element_type=F32)


def dot_nt(lhs, rhs):
    return lax.dot_general(lhs, rhs, (((1,), (1,)), ((), ())), preferred_element_type=F32)


def norm(values, scaling):
    inverse = lax.rsqrt(jnp.mean(values * values, axis=-1, keepdims=True) + NORM_EPS)
    return (values * inverse * scaling).astype(BF)


def silu(values):
    half = 0.5 * values
    return half + half * jnp.tanh(half)


def parts_of(values, count):
    parts = []
    for _ in range(count):
        part = values.astype(BF)
        parts.append(part)
        values = values - part.astype(F32)
    return parts


def padded(rows):
    return -(-rows // 256) * 256


def gains(noise_ref, w_cond_ref, layer):
    return 1.0 + jnp.dot(
        noise_ref[...], w_cond_ref[layer], precision=lax.Precision.HIGHEST, preferred_element_type=F32
    )


def link_offsets(links, first, node_total):
    own = first + lax.broadcasted_iota(jnp.int32, links.shape, 1)
    away = links - own
    away = jnp.where(away > node_total // 2, away - node_total, away)
    away = jnp.where(away < -(node_total // 2), away + node_total, away)
    return away.astype(F32)


def count_matrix(offsets, width):
    link_count, rows = offsets.shape
    places = offsets + (WIN + lax.broadcasted_iota(jnp.int32, offsets.shape, 1)).astype(F32)
    places = jnp.concatenate([places, jnp.full((128 - link_count, rows), -1.0, F32)], axis=0).T
    columns = lax.broadcasted_iota(jnp.int32, (rows, width), 1).astype(F32)
    total = jnp.zeros((rows, width), F32)
    for slot in range(link_count):
        total = total + jnp.where(columns == places[:, slot : slot + 1], 1.0, 0.0)
    return total.astype(BF)


def layer(values, normed, window, counts, w_in, w_out, link_count):
    neighbours = (dot(counts, window)[: values.shape[0]] * (1.0 / link_count)).astype(BF)
    depth = normed.shape[1]
    preact = dot(normed, w_in[:depth]) + dot(neighbours, w_in[depth:])
    return values + dot(silu(preact).astype(BF), w_out)


def pack_kernel(node_total, place, latent, links, near, far):
    odd, first = place[0], place[1]
    halo = 2 * WIN
    rows = latent.shape[1]
    offsets = link_offsets(links[...], first, node_total).astype(BF)
    for send, start in ((near, (1 - odd) * (rows - halo)), (far, odd * (rows - halo))):
        start = pl.multiple_of(start, 64)
        for member in range(latent.shape[0]):
            send[member * halo : (member + 1) * halo] = latent[member, pl.ds(start, halo)]
        tail = latent.shape[0] * halo
        send[tail:] = jnp.zeros((send.shape[0] - tail, send.shape[1]), BF)
        send[tail : tail + offsets.shape[0], : offsets.shape[1]] = offsets


def received_offsets(received, tail, link_count, rows):
    return received[tail : tail + 16, :rows].astype(F32)[:link_count]


def near_kernel(
    node_total, place, latent, links, near, noise, w_cond, w_in, w_out,
    state_out, normed_own_out, normed_next_out, counts_out, window, inputs
):
    odd, first = place[0], place[1]
    members, rows, _ = latent.shape
    link_count = links.shape[0]
    halo = 2 * WIN
    own_at = pl.multiple_of(odd * halo, 64)
    near_at = pl.multiple_of((1 - odd) * rows, 64)
    scaling = gains(noise, w_cond, 0)
    next_scaling = gains(noise, w_cond, 1)
    own_offsets = link_offsets(links[...], first, node_total)
    near_offsets = received_offsets(near, members * halo, link_count, rows)
    lane = lax.broadcasted_iota(jnp.int32, own_offsets.shape, 1)
    mine = jnp.logical_and(lane >= (1 - odd) * WIN, lane < rows - odd * WIN)
    mixed = jnp.where(mine, own_offsets, near_offsets)
    mixed = pltpu.roll(mixed, rows - WIN - odd * (rows - 2 * WIN), 1)
    counts = count_matrix(mixed, window.shape[1])
    counts_out[...] = count_matrix(own_offsets, window.shape[1])
    for member in range(members):
        scale = scaling[member : member + 1]
        own = latent[member]
        edge = near[member * halo : (member + 1) * halo]
        inputs[member, pl.ds(own_at, rows)] = own
        inputs[member, pl.ds(near_at, halo)] = edge
        normed_own = norm(own.astype(F32), scale)
        normed_own_out[member] = normed_own
        window[member, rows + halo :] = jnp.zeros((window.shape[1] - rows - halo, window.shape[2]), BF)
        window[member, pl.ds(own_at, rows)] = normed_own
        window[member, pl.ds(near_at, halo)] = norm(edge.astype(F32), scale)
        values = inputs[member, WIN : WIN + rows].astype(F32)
        values = layer(
            values, window[member, WIN : WIN + rows], window[member], counts, w_in[0], w_out[0], link_count
        )
        state_out[member] = values
        normed_next_out[member] = norm(values, next_scaling[member : member + 1])


def far_kernel(
    node_total, copies, place, latent, links, far, noise, w_cond, w_in, w_out, dec_gain, w_dec,
    state_in, normed_own, normed_next, counts_own, decoded_out, send_out,
    window, inputs, state, window_next, features,
):
    odd, first = place[0], place[1]
    members, rows, _ = latent.shape
    link_count = links.shape[0]
    halo = 2 * WIN
    even = 1 - odd
    scaling = gains(noise, w_cond, 0)
    next_scaling = gains(noise, w_cond, 1)
    own_offsets = link_offsets(links[...], first, node_total)
    far_offsets = received_offsets(far, members * halo, link_count, rows)
    lane = lax.broadcasted_iota(jnp.int32, own_offsets.shape, 1)
    mine = jnp.logical_or(
        jnp.logical_and(odd == 0, lane < WIN), jnp.logical_and(odd == 1, lane >= rows - WIN)
    )
    counts = count_matrix(pltpu.roll(jnp.where(mine, own_offsets, far_offsets), WIN, 1), window.shape[1])
    filled = rows + halo
    for member in range(members):
        window[member, 2 * halo :] = jnp.zeros((window.shape[1] - 2 * halo, window.shape[2]), BF)
        window_next[member, filled:] = jnp.zeros((window_next.shape[1] - filled, window_next.shape[2]), BF)
        edge = far[member * halo : (member + 1) * halo]
        window[member, pl.ds(pl.multiple_of(odd * halo, 64), halo)] = norm(
            edge.astype(F32), scaling[member : member + 1]
        )
        window[member, pl.ds(pl.multiple_of(even * halo, 64), halo)] = normed_own[
            member, pl.ds(pl.multiple_of(odd * (rows - halo), 64), halo)
        ]
        inputs[member, pl.ds(pl.multiple_of(odd * WIN, 32), WIN)] = far[
            pl.ds(pl.multiple_of(member * halo + even * WIN, 32), WIN)
        ]
        inputs[member, pl.ds(pl.multiple_of(even * WIN, 32), WIN)] = latent[
            member, pl.ds(pl.multiple_of(odd * (rows - WIN), 32), WIN)
        ]
        values = layer(
            inputs[member].astype(F32), window[member, WIN : WIN + halo], window[member], counts, w_in[0], w_out[0], link_count
        )
        far_at = pl.multiple_of(odd * rows, 64)
        near_at = pl.multiple_of(even * halo, 64)
        state[member, pl.ds(far_at, halo)] = values
        state[member, pl.ds(near_at, rows)] = state_in[member]
        window_next[member, pl.ds(far_at, halo)] = norm(values, next_scaling[member : member + 1])
        window_next[member, pl.ds(near_at, rows)] = normed_next[member]
        values = layer(
            state[member, WIN : WIN + rows], window_next[member, WIN : WIN + rows], window_next[member], counts_own[...],
            w_in[1], w_out[1], link_count,
        )
        features[member * rows : (member + 1) * rows] = norm(values, dec_gain[...])
    decoded = dot_nt(w_dec[...], features[...])
    decoded_out[...] = decoded
    rounded = decoded.astype(BF)
    for copy in range(copies):
        send_out[copy] = rounded


def grid_kernel(ensemble, place, decoded, prior, target, vertex, weight, incidence_out, base_out):
    nodes, points = incidence_out.shape
    ids = place[1] + lax.broadcasted_iota(jnp.int32, (nodes, points), 0)
    incidence = jnp.where(ids == vertex[...], 1.0, 0.0).astype(BF)
    incidence_out[...] = incidence
    before = prior[...].astype(F32)
    truth = target[...].astype(F32)
    for member in range(base_out.shape[0]):
        own = decoded[:, member * nodes : (member + 1) * nodes]
        at_points = sum(dot(part, incidence) for part in parts_of(own, 3)[::-1])
        missed = (before + at_points).astype(BF).astype(F32) - truth
        reached = lax.rsqrt(jnp.sum(missed * missed, axis=0, keepdims=True) + DIST_EPS)
        base_out[member] = missed * (reached * weight[...] * (1.0 / ensemble))


def score_kernel(ensemble, decoded, others, incidence, base, weight, w_dec, grad_out, vertex_out):
    members, channels, _ = base.shape
    nodes = incidence.shape[0]
    factor = weight[...] * (1.0 / (ensemble * (ensemble - 1)))
    step = 128
    for member in range(members):
        pulls = []
        for start in range(member * nodes, (member + 1) * nodes, step):
            anchor = decoded[:, start : start + step].astype(BF).astype(F32)
            total = jnp.zeros_like(anchor)
            for group in range(others.shape[0]):
                for at in range(start % nodes, members * nodes, nodes):
                    offset = anchor - others[group, :, at : at + step].astype(F32)
                    near = jnp.sum(offset * offset, axis=0, keepdims=True) + DIST_EPS
                    total = total + offset * lax.rsqrt(near)
            pulls.append(total)
        pull = jnp.concatenate(pulls, axis=1)
        at_points = sum(dot(part, incidence[...]) for part in parts_of(pull, 2)[::-1])
        grad = (base[member] - factor * at_points).astype(BF)
        grad_out[member] = grad
        by_node = dot_nt(incidence[...], grad)
        vertex_out[member] = sum(dot(part, w_dec[...]) for part in parts_of(by_node, 3)[::-1]).astype(BF)


def call(kernel, outs, count, scratch=(), place=True):
    return pl.pallas_call(
        kernel,
        out_shape=[jax.ShapeDtypeStruct(shape, kind) for shape, kind in outs],
        in_specs=[SMEM] * place + [VMEM] * count,
        out_specs=[VMEM] * len(outs),
        scratch_shapes=[pltpu.VMEM(shape, kind) for shape, kind in scratch],
        compiler_params=PARAMS,
    )


def per_device(
    latent, noise_draw, mesh_links, w_cond, w_in, w_out, dec_gain, w_dec,
    target_vertex_map, prior_field, target, location_loss_factor,
):
    members, rows, depth = latent.shape
    channels, points = prior_field.shape
    shards = lax.axis_size("node")
    groups = lax.axis_size("member")
    ensemble = members * groups
    node_total = rows * shards
    halo = 2 * WIN
    wide = padded(rows + halo)
    shard = lax.axis_index("node")
    place = jnp.stack([shard % 2, shard * rows]).astype(jnp.int32)
    sent = (members * halo + 16, depth)
    near_pairs = [(i, i ^ 1) for i in range(shards)]
    far_pairs = [(i, (i + 1) % shards if i % 2 else (i - 1) % shards) for i in range(shards)]

    near, far = call(functools.partial(pack_kernel, node_total), [(sent, BF)] * 2, 2)(place, latent, mesh_links)
    far = lax.ppermute(far, "node", far_pairs)
    near = lax.ppermute(near, "node", near_pairs)
    state, normed_own, normed_next, counts_own = call(
        functools.partial(near_kernel, node_total),
        [
            ((members, rows, depth), F32),
            ((members, rows, depth), BF),
            ((members, rows, depth), BF),
            ((rows, wide), BF),
        ],
        7,
        [((members, wide, depth), BF), ((members, rows + halo, depth), BF)],
    )(place, latent, mesh_links, near, noise_draw, w_cond, w_in, w_out)
    decoded, send = call(
        functools.partial(far_kernel, node_total, groups),
        [((channels, members * rows), F32), ((groups, channels, members * rows), BF)],
        13,
        [
            ((members, padded(2 * halo), depth), BF),
            ((members, halo, depth), BF),
            ((members, rows + halo, depth), F32),
            ((members, wide, depth), BF),
            ((members * rows, depth), BF),
        ],
    )(
        place, latent, mesh_links, far, noise_draw, w_cond, w_in, w_out, dec_gain.reshape(1, depth), w_dec,
        state, normed_own, normed_next, counts_own,
    )
    others = lax.all_to_all(send, "member", split_axis=0, concat_axis=0, tiled=True)
    weight = location_loss_factor.reshape(1, points)
    incidence, base = call(
        functools.partial(grid_kernel, ensemble),
        [((rows, points), BF), ((members, channels, points), F32)],
        5,
    )(place, decoded, prior_field, target, target_vertex_map.reshape(1, points), weight)
    prediction_sensitivity, vertex_attribute_sensitivity = call(
        functools.partial(score_kernel, ensemble),
        [((members, channels, points), BF), ((members, rows, depth), BF)],
        6,
        place=False,
    )(decoded, others, incidence, base, weight, w_dec)
    return prediction_sensitivity, vertex_attribute_sensitivity


def solution(mesh):
    in_specs = (
        P("member", "node", None),
        P("member", None),
        P(None, "node"),
        P(),
        P(),
        P(),
        P(),
        P(),
        P("node"),
        P(None, "node"),
        P(None, "node"),
        P("node"),
    )
    out_specs = (P("member", None, "node"), P("member", "node", None))
    return jax.shard_map(
        per_device, mesh=mesh, in_specs=in_specs, out_specs=out_specs, check_vma=False
    )
```

```python
import functools

import jax
import jax.numpy as jnp
from jax import lax
from jax.experimental import pallas as pl
from jax.experimental.pallas import tpu as pltpu
from jax.sharding import PartitionSpec as P

WIN = 96
NORM_EPS = 1e-06
DIST_EPS = 1e-06

BF = jnp.bfloat16
F32 = jnp.float32
VMEM = pl.BlockSpec(memory_space=pltpu.VMEM)
SMEM = pl.BlockSpec(memory_space=pltpu.SMEM)
HBM = pl.BlockSpec(memory_space=pltpu.HBM)
PARAMS = pltpu.CompilerParams(vmem_limit_bytes=40 * 2**20)


def dot(lhs, rhs):
    return jnp.dot(lhs, rhs, preferred_element_type=F32)


def dot_nt(lhs, rhs):
    return lax.dot_general(lhs, rhs, (((1,), (1,)), ((), ())), preferred_element_type=F32)


def norm(values, scaling):
    inverse = lax.rsqrt(jnp.mean(values * values, axis=-1, keepdims=True) + NORM_EPS)
    return (values * inverse * scaling).astype(BF)


def silu(values):
    half = 0.5 * values
    return half + half * jnp.tanh(half)


def parts_of(values, count):
    parts = []
    for _ in range(count):
        part = values.astype(BF)
        parts.append(part)
        values = values - part.astype(F32)
    return parts


def padded(rows):
    return -(-rows // 256) * 256


def gains(noise_ref, w_cond_ref, layer):
    return 1.0 + jnp.dot(
        noise_ref[...], w_cond_ref[layer], precision=lax.Precision.HIGHEST, preferred_element_type=F32
    )


def link_offsets(links, first, node_total):
    own = first + lax.broadcasted_iota(jnp.int32, links.shape, 1)
    away = links - own
    away = jnp.where(away > node_total // 2, away - node_total, away)
    away = jnp.where(away < -(node_total // 2), away + node_total, away)
    return away.astype(F32)


def count_matrix(offsets, width):
    link_count, rows = offsets.shape
    places = offsets + (WIN + lax.broadcasted_iota(jnp.int32, offsets.shape, 1)).astype(F32)
    places = jnp.concatenate([places, jnp.full((128 - link_count, rows), -1.0, F32)], axis=0).T
    columns = lax.broadcasted_iota(jnp.int32, (rows, width), 1).astype(F32)
    total = jnp.zeros((rows, width), F32)
    for slot in range(link_count):
        total = total + jnp.where(columns == places[:, slot : slot + 1], 1.0, 0.0)
    return total.astype(BF)


def layer(values, normed, window, counts, w_in, w_out, link_count):
    neighbours = (dot(counts, window)[: values.shape[0]] * (1.0 / link_count)).astype(BF)
    depth = normed.shape[1]
    preact = dot(normed, w_in[:depth]) + dot(neighbours, w_in[depth:])
    return values + dot(silu(preact).astype(BF), w_out)


def fetch_all(pairs, sems):
    fetches = [pltpu.make_async_copy(there, here, sems.at[at]) for at, (there, here) in enumerate(pairs)]
    for fetch in fetches:
        fetch.start()
    return fetches


def pack_kernel(node_total, place, latent, links_in, near, far, links, sems):
    odd, first = place[0], place[1]
    halo = 2 * WIN
    members, rows, _ = latent.shape
    pairs = [(links_in, links)]
    for send, start in ((near, (1 - odd) * (rows - halo)), (far, odd * (rows - halo))):
        start = pl.multiple_of(start, 64)
        for member in range(members):
            pairs.append((latent.at[member, pl.ds(start, halo)], send.at[pl.ds(member * halo, halo)]))
    fetches = fetch_all(pairs, sems)
    fetches[0].wait()
    offsets = link_offsets(links[...], first, node_total).astype(BF)
    tail = members * halo
    for send in (near, far):
        send[tail:] = jnp.zeros((send.shape[0] - tail, send.shape[1]), BF)
        send[tail : tail + offsets.shape[0], : offsets.shape[1]] = offsets
    for fetch in fetches[1:]:
        fetch.wait()


def received_offsets(received, tail, link_count, rows):
    return received[tail : tail + 16, :rows].astype(F32)[:link_count]


def near_kernel(
    node_total, place, near, links_in, noise_in, w_cond_in, latent_in, w_in_in, w_out_in,
    state_out, normed_own_out, normed_next_out, counts_out, window, inputs,
    links, noise, w_cond, latent, w_in, w_out, sems
):
    fetches = fetch_all(
        (
            (links_in, links),
            (noise_in, noise),
            (w_cond_in, w_cond),
            (latent_in, latent),
            (w_in_in.at[0], w_in),
            (w_out_in.at[0], w_out),
        ),
        sems,
    )
    odd, first = place[0], place[1]
    members, rows, _ = latent.shape
    link_count = links.shape[0]
    halo = 2 * WIN
    own_at = pl.multiple_of(odd * halo, 64)
    near_at = pl.multiple_of((1 - odd) * rows, 64)
    fetches[0].wait()
    own_offsets = link_offsets(links[...], first, node_total)
    near_offsets = received_offsets(near, members * halo, link_count, rows)
    lane = lax.broadcasted_iota(jnp.int32, own_offsets.shape, 1)
    mine = jnp.logical_and(lane >= (1 - odd) * WIN, lane < rows - odd * WIN)
    mixed = jnp.where(mine, own_offsets, near_offsets)
    mixed = pltpu.roll(mixed, rows - WIN - odd * (rows - 2 * WIN), 1)
    counts = count_matrix(mixed, window.shape[1])
    counts_out[...] = count_matrix(own_offsets, window.shape[1])
    for fetch in fetches[1:4]:
        fetch.wait()
    scaling = gains(noise, w_cond, 0)
    next_scaling = gains(noise, w_cond, 1)
    for member in range(members):
        scale = scaling[member : member + 1]
        own = latent[member]
        edge = near[member * halo : (member + 1) * halo]
        inputs[member, pl.ds(own_at, rows)] = own
        inputs[member, pl.ds(near_at, halo)] = edge
        normed_own = norm(own.astype(F32), scale)
        normed_own_out[member] = normed_own
        window[member, rows + halo :] = jnp.zeros((window.shape[1] - rows - halo, window.shape[2]), BF)
        window[member, pl.ds(own_at, rows)] = normed_own
        window[member, pl.ds(near_at, halo)] = norm(edge.astype(F32), scale)
    for fetch in fetches[4:]:
        fetch.wait()
    for member in range(members):
        values = inputs[member, WIN : WIN + rows].astype(F32)
        values = layer(
            values, window[member, WIN : WIN + rows], window[member], counts,
            w_in[...], w_out[...], link_count,
        )
        state_out[member] = values
        normed_next_out[member] = norm(values, next_scaling[member : member + 1])


def far_kernel(
    node_total, place, latent, links, far, noise, w_cond, w_in, w_out, dec_gain, w_dec,
    state_in, normed_own, normed_next, counts_own, decoded_out, rounded_out,
    window, inputs, state, window_next, features,
):
    odd, first = place[0], place[1]
    members, rows, _ = latent.shape
    link_count = links.shape[0]
    halo = 2 * WIN
    even = 1 - odd
    scaling = gains(noise, w_cond, 0)
    next_scaling = gains(noise, w_cond, 1)
    own_offsets = link_offsets(links[...], first, node_total)
    far_offsets = received_offsets(far, members * halo, link_count, rows)
    lane = lax.broadcasted_iota(jnp.int32, own_offsets.shape, 1)
    mine = jnp.logical_or(
        jnp.logical_and(odd == 0, lane < WIN), jnp.logical_and(odd == 1, lane >= rows - WIN)
    )
    counts = count_matrix(pltpu.roll(jnp.where(mine, own_offsets, far_offsets), WIN, 1), window.shape[1])
    filled = rows + halo
    for member in range(members):
        window[member, 2 * halo :] = jnp.zeros((window.shape[1] - 2 * halo, window.shape[2]), BF)
        window_next[member, filled:] = jnp.zeros((window_next.shape[1] - filled, window_next.shape[2]), BF)
        edge = far[member * halo : (member + 1) * halo]
        window[member, pl.ds(pl.multiple_of(odd * halo, 64), halo)] = norm(
            edge.astype(F32), scaling[member : member + 1]
        )
        window[member, pl.ds(pl.multiple_of(even * halo, 64), halo)] = normed_own[
            member, pl.ds(pl.multiple_of(odd * (rows - halo), 64), halo)
        ]
        inputs[member, pl.ds(pl.multiple_of(odd * WIN, 32), WIN)] = far[
            pl.ds(pl.multiple_of(member * halo + even * WIN, 32), WIN)
        ]
        inputs[member, pl.ds(pl.multiple_of(even * WIN, 32), WIN)] = latent[
            member, pl.ds(pl.multiple_of(odd * (rows - WIN), 32), WIN)
        ]
        values = layer(
            inputs[member].astype(F32), window[member, WIN : WIN + halo], window[member], counts, w_in[0], w_out[0], link_count
        )
        far_at = pl.multiple_of(odd * rows, 64)
        near_at = pl.multiple_of(even * halo, 64)
        state[member, pl.ds(far_at, halo)] = values
        state[member, pl.ds(near_at, rows)] = state_in[member]
        window_next[member, pl.ds(far_at, halo)] = norm(values, next_scaling[member : member + 1])
        window_next[member, pl.ds(near_at, rows)] = normed_next[member]
        values = layer(
            state[member, WIN : WIN + rows], window_next[member, WIN : WIN + rows], window_next[member], counts_own[...],
            w_in[1], w_out[1], link_count,
        )
        features[member * rows : (member + 1) * rows] = norm(values, dec_gain[...])
    decoded = dot_nt(w_dec[...], features[...])
    decoded_out[...] = decoded
    rounded_out[...] = decoded.astype(BF)


def stack_kernel(mine, partner, out):
    wide = mine.shape[1]
    for copy in range(out.shape[0]):
        out[copy, :, :wide] = mine[...]
        out[copy, :, wide:] = partner[...]


def grid_kernel(ensemble, place, decoded, prior, target, vertex, weight, incidence_out, base_out):
    nodes, points = incidence_out.shape
    ids = place[1] + lax.broadcasted_iota(jnp.int32, (nodes, points), 0)
    incidence = jnp.where(ids == vertex[...], 1.0, 0.0).astype(BF)
    incidence_out[...] = incidence
    before = prior[...].astype(F32)
    truth = target[...].astype(F32)
    for member in range(base_out.shape[0]):
        own = decoded[:, member * nodes : (member + 1) * nodes]
        at_points = sum(dot(part, incidence) for part in parts_of(own, 3)[::-1])
        missed = (before + at_points).astype(BF).astype(F32) - truth
        reached = lax.rsqrt(jnp.sum(missed * missed, axis=0, keepdims=True) + DIST_EPS)
        base_out[member] = missed * (reached * weight[...] * (1.0 / ensemble))


def score_kernel(
    ensemble, rounded, others, incidence, base, weight, w_dec, grad_out, vertex_out, grads, vertices, sems
):
    members, channels, _ = base.shape
    nodes = incidence.shape[0]
    factor = weight[...] * (1.0 / (ensemble * (ensemble - 1)))
    step = 128
    copies = []
    for member in range(members):
        pulls = []
        for start in range(member * nodes, (member + 1) * nodes, step):
            anchor = rounded[:, start : start + step].astype(F32)
            total = jnp.zeros_like(anchor)
            for group in range(others.shape[0]):
                for at in range(start % nodes, others.shape[2], nodes):
                    offset = anchor - others[group, :, at : at + step].astype(F32)
                    near = jnp.sum(offset * offset, axis=0, keepdims=True) + DIST_EPS
                    total = total + offset * lax.rsqrt(near)
            pulls.append(total)
        pull = jnp.concatenate(pulls, axis=1)
        at_points = sum(dot(part, incidence[...]) for part in parts_of(pull, 2)[::-1])
        grad = (base[member] - factor * at_points).astype(BF)
        grads[member] = grad
        copies.append(pltpu.make_async_copy(grads.at[member], grad_out.at[member], sems.at[0, member]))
        copies[-1].start()
        by_node = dot_nt(incidence[...], grad)
        vertices[member] = sum(dot(part, w_dec[...]) for part in parts_of(by_node, 3)[::-1]).astype(BF)
        copies.append(pltpu.make_async_copy(vertices.at[member], vertex_out.at[member], sems.at[1, member]))
        copies[-1].start()
    for copy in copies:
        copy.wait()


def call(kernel, outs, ins, scratch=(), out_spec=VMEM):
    return pl.pallas_call(
        kernel,
        out_shape=[jax.ShapeDtypeStruct(shape, kind) for shape, kind in outs],
        in_specs=ins,
        out_specs=[out_spec] * len(outs),
        scratch_shapes=[pltpu.VMEM(*spec) if isinstance(spec, tuple) else spec for spec in scratch],
        compiler_params=PARAMS,
    )


def per_device(
    latent, noise_draw, mesh_links, w_cond, w_in, w_out, dec_gain, w_dec,
    target_vertex_map, prior_field, target, location_loss_factor,
):
    members, rows, depth = latent.shape
    channels, points = prior_field.shape
    shards = lax.axis_size("node")
    groups = lax.axis_size("member")
    ensemble = members * groups
    node_total = rows * shards
    halo = 2 * WIN
    wide = padded(rows + halo)
    shard = lax.axis_index("node")
    place = jnp.stack([shard % 2, shard * rows]).astype(jnp.int32)
    sent = (members * halo + 16, depth)
    near_pairs = [(i, i ^ 1) for i in range(shards)]
    far_pairs = [(i, (i + 1) % shards if i % 2 else (i - 1) % shards) for i in range(shards)]

    dma = pltpu.SemaphoreType.DMA

    in_hbm = functools.partial(pltpu.with_memory_space_constraint, memory_space=pltpu.HBM)

    near, far = call(
        functools.partial(pack_kernel, node_total), [(sent, BF)] * 2, [SMEM, HBM, HBM], [(mesh_links.shape, jnp.int32), dma((1 + 2 * members,))]
    )(place, in_hbm(latent), in_hbm(mesh_links))
    far = lax.ppermute(far, "node", far_pairs)
    near = lax.ppermute(near, "node", near_pairs)
    state, normed_own, normed_next, counts_own = call(
        functools.partial(near_kernel, node_total),
        [
            ((members, rows, depth), F32),
            ((members, rows, depth), BF),
            ((members, rows, depth), BF),
            ((rows, wide), BF),
        ],
        [SMEM, VMEM] + [HBM] * 6,
        [
            ((members, wide, depth), BF),
            ((members, rows + halo, depth), BF),
            (mesh_links.shape, jnp.int32),
            (noise_draw.shape, F32),
            (w_cond.shape, F32),
            (latent.shape, BF),
            (w_in.shape[1:], BF),
            (w_out.shape[1:], BF),
            dma((6,)),
        ],
    )(place, near, *map(in_hbm, (mesh_links, noise_draw, w_cond, latent, w_in, w_out)))
    decoded, rounded = call(
        functools.partial(far_kernel, node_total),
        [((channels, members * rows), F32), ((channels, members * rows), BF)],
        [SMEM] + [VMEM] * 13,
        [
            ((members, padded(2 * halo), depth), BF),
            ((members, halo, depth), BF),
            ((members, rows + halo, depth), F32),
            ((members, wide, depth), BF),
            ((members * rows, depth), BF),
        ],
    )(
        place, latent, mesh_links, far, noise_draw, w_cond, w_in, w_out, dec_gain.reshape(1, depth), w_dec,
        state, normed_own, normed_next, counts_own,
    )
    partner = lax.ppermute(rounded, "member", [(i, i ^ 1) for i in range(groups)])
    weight = location_loss_factor.reshape(1, points)
    incidence, base = call(
        functools.partial(grid_kernel, ensemble),
        [((rows, points), BF), ((members, channels, points), F32)],
        [SMEM] + [VMEM] * 5,
    )(place, decoded, prior_field, target, target_vertex_map.reshape(1, points), weight)
    partner, base = lax.optimization_barrier((partner, base))
    (stacked,) = call(
        stack_kernel, [((groups // 2, channels, 2 * members * rows), BF)], [VMEM] * 2
    )(rounded, partner)
    others = lax.all_to_all(
        stacked, "member", split_axis=0, concat_axis=0, tiled=True,
        axis_index_groups=[list(range(half, groups, 2)) for half in range(2)],
    )
    return call(
        functools.partial(score_kernel, ensemble),
        [((members, channels, points), BF), ((members, rows, depth), BF)],
        [VMEM] * 6,
        [((members, channels, points), BF), ((members, rows, depth), BF), dma((2, members))],
        HBM,
    )(rounded, others, incidence, base, weight, w_dec)


def solution(mesh):
    in_specs = (
        P("member", "node", None),
        P("member", None),
        P(None, "node"),
        P(),
        P(),
        P(),
        P(),
        P(),
        P("node"),
        P(None, "node"),
        P(None, "node"),
        P("node"),
    )
    out_specs = (P("member", None, "node"), P("member", "node", None))
    return jax.shard_map(
        per_device, mesh=mesh, in_specs=in_specs, out_specs=out_specs, check_vma=False
    )
```

```python
import functools

import jax
import jax.numpy as jnp
from jax import lax
from jax.experimental import pallas as pl
from jax.experimental.pallas import tpu as pltpu
from jax.sharding import PartitionSpec as P

WIN = 96
NORM_EPS = 1e-06
DIST_EPS = 1e-06

LONG = 10**11

BF = jnp.bfloat16
F32 = jnp.float32
VMEM = pl.BlockSpec(memory_space=pltpu.VMEM)
HBM = pl.BlockSpec(memory_space=pltpu.HBM)
PARAMS = pltpu.CompilerParams(vmem_limit_bytes=40 * 2**20)


def dot(lhs, rhs):
    return jnp.dot(lhs, rhs, preferred_element_type=F32)


def dot_nt(lhs, rhs):
    return lax.dot_general(lhs, rhs, (((1,), (1,)), ((), ())), preferred_element_type=F32)


def norm(values, scaling):
    inverse = lax.rsqrt(jnp.mean(values * values, axis=-1, keepdims=True) + NORM_EPS)
    return (values * inverse * scaling).astype(BF)


def silu(values):
    half = 0.5 * values
    return half + half * jnp.tanh(half)


def parts_of(values, count):
    parts = []
    for _ in range(count):
        part = values.astype(BF)
        parts.append(part)
        values = values - part.astype(F32)
    return parts


def padded(rows):
    return -(-rows // 256) * 256


def gains(noise_ref, w_cond_ref, layer):
    return 1.0 + jnp.dot(
        noise_ref[...], w_cond_ref[layer], precision=lax.Precision.HIGHEST, preferred_element_type=F32
    )


def link_offsets(links, first, node_total):
    own = first + lax.broadcasted_iota(jnp.int32, links.shape, 1)
    away = links - own
    away = jnp.where(away > node_total // 2, away - node_total, away)
    away = jnp.where(away < -(node_total // 2), away + node_total, away)
    return away.astype(F32)


def count_matrix(offsets, width):
    link_count, rows = offsets.shape
    places = offsets + (WIN + lax.broadcasted_iota(jnp.int32, offsets.shape, 1)).astype(F32)
    places = jnp.concatenate([places, jnp.full((128 - link_count, rows), -1.0, F32)], axis=0).T
    columns = lax.broadcasted_iota(jnp.int32, (rows, width), 1).astype(F32)
    total = jnp.zeros((rows, width), F32)
    for slot in range(link_count):
        total = total + jnp.where(columns == places[:, slot : slot + 1], 1.0, 0.0)
    return total.astype(BF)


def layer(values, normed, windows, counts, w_in, w_out, link_count):
    rows = values.shape[0] // len(windows)
    sums = [dot(counts, window)[:rows] for window in windows]
    neighbours = (jnp.concatenate(sums, axis=0) * (1.0 / link_count)).astype(BF)
    depth = normed.shape[1]
    preact = dot(normed, w_in[:depth]) + dot(neighbours, w_in[depth:])
    return values + dot(silu(preact).astype(BF), w_out)


def rows_of(array, start, count):
    return jnp.concatenate([array[member, start : start + count] for member in range(array.shape[0])], axis=0)


def position(shards, rows):
    shard = lax.axis_index("node")
    return lax.rem(shard, 2), shard * rows, shards * rows


def fetch_all(pairs, sems):
    fetches = [pltpu.make_async_copy(there, here, sems.at[at]) for at, (there, here) in enumerate(pairs)]
    for fetch in fetches:
        fetch.start()
    return fetches


def pack_kernel(shards, latent, links_in, near, far, links, sems):
    halo = 2 * WIN
    members, rows, _ = latent.shape
    odd, first, node_total = position(shards, rows)
    pairs = [(links_in, links)]
    for send, start in ((near, (1 - odd) * (rows - halo)), (far, odd * (rows - halo))):
        start = pl.multiple_of(start, 64)
        for member in range(members):
            pairs.append((latent.at[member, pl.ds(start, halo)], send.at[pl.ds(member * halo, halo)]))
    fetches = fetch_all(pairs, sems)
    fetches[0].wait()
    offsets = link_offsets(links[...], first, node_total).astype(BF)
    tail = members * halo
    for send in (near, far):
        send[tail:] = jnp.zeros((send.shape[0] - tail, send.shape[1]), BF)
        send[tail : tail + offsets.shape[0], : offsets.shape[1]] = offsets
    for fetch in fetches[1:]:
        fetch.wait()


def received_offsets(received, tail, link_count, rows):
    return received[tail : tail + 16, :rows].astype(F32)[:link_count]


def near_kernel(
    shards, near, links_in, noise_in, w_cond_in, latent_in, vertex_in, w_in_in, w_out_in,
    state_out, normed_own_out, normed_next_out, counts_out, scaling_out, incidence_out, window, inputs,
    links, noise, w_cond, latent, vertex, w_in, w_out, sems
):
    fetches = fetch_all(
        (
            (links_in, links),
            (noise_in, noise),
            (w_cond_in, w_cond),
            (latent_in, latent),
            (vertex_in, vertex),
            (w_in_in.at[0], w_in),
            (w_out_in.at[0], w_out),
        ),
        sems,
    )
    members, rows, _ = latent.shape
    odd, first, node_total = position(shards, rows)
    link_count = links.shape[0]
    halo = 2 * WIN
    own_at = pl.multiple_of(odd * halo, 64)
    near_at = pl.multiple_of((1 - odd) * rows, 64)
    fetches[0].wait()
    own_offsets = link_offsets(links[...], first, node_total)
    near_offsets = received_offsets(near, members * halo, link_count, rows)
    lane = lax.broadcasted_iota(jnp.int32, own_offsets.shape, 1)
    mine = jnp.logical_and(lane >= (1 - odd) * WIN, lane < rows - odd * WIN)
    mixed = jnp.where(mine, own_offsets, near_offsets)
    mixed = pltpu.roll(mixed, rows - WIN - odd * (rows - 2 * WIN), 1)
    counts = count_matrix(mixed, window.shape[1])
    counts_out[...] = count_matrix(own_offsets, window.shape[1])
    for fetch in fetches[1:5]:
        fetch.wait()
    scaling = gains(noise, w_cond, 0)
    next_scaling = gains(noise, w_cond, 1)
    scaling_out[0] = scaling
    scaling_out[1] = next_scaling
    for member in range(members):
        scale = scaling[member : member + 1]
        own = latent[member]
        edge = near[member * halo : (member + 1) * halo]
        inputs[member, pl.ds(own_at, rows)] = own
        inputs[member, pl.ds(near_at, halo)] = edge
        normed_own = norm(own.astype(F32), scale)
        normed_own_out[member] = normed_own
        window[member, rows + halo :] = jnp.zeros((window.shape[1] - rows - halo, window.shape[2]), BF)
        window[member, pl.ds(own_at, rows)] = normed_own
        window[member, pl.ds(near_at, halo)] = norm(edge.astype(F32), scale)
    for fetch in fetches[5:]:
        fetch.wait()
    values = layer(
        rows_of(inputs, WIN, rows).astype(F32), rows_of(window, WIN, rows), [window[m] for m in range(members)],
        counts, w_in[...], w_out[...], link_count,
    )
    for member in range(members):
        own = values[member * rows : (member + 1) * rows]
        state_out[member] = own
        normed_next_out[member] = norm(own, next_scaling[member : member + 1])
    ids = first + lax.broadcasted_iota(jnp.int32, incidence_out.shape, 0)
    incidence_out[...] = jnp.where(ids == vertex[...], 1.0, 0.0).astype(BF)


def far_kernel(
    shards, latent, links, far, scaling, w_in, w_out, dec_gain, w_dec,
    state_in, normed_own, normed_next, counts_own, decoded_out, rounded_out,
    window, inputs, state, window_next,
):
    members, rows, _ = latent.shape
    odd, first, node_total = position(shards, rows)
    even = 1 - odd
    link_count = links.shape[0]
    halo = 2 * WIN
    filled = rows + halo
    own_offsets = link_offsets(links[...], first, node_total)
    far_offsets = received_offsets(far, members * halo, link_count, rows)
    lane = lax.broadcasted_iota(jnp.int32, own_offsets.shape, 1)
    mine = jnp.logical_or(
        jnp.logical_and(odd == 0, lane < WIN), jnp.logical_and(odd == 1, lane >= rows - WIN)
    )
    counts = count_matrix(pltpu.roll(jnp.where(mine, own_offsets, far_offsets), WIN, 1), window.shape[1])
    far_at = pl.multiple_of(odd * rows, 64)
    near_at = pl.multiple_of(even * halo, 64)
    for member in range(members):
        window[member, 2 * halo :] = jnp.zeros((window.shape[1] - 2 * halo, window.shape[2]), BF)
        window_next[member, filled:] = jnp.zeros((window_next.shape[1] - filled, window_next.shape[2]), BF)
        edge = far[member * halo : (member + 1) * halo]
        window[member, pl.ds(pl.multiple_of(odd * halo, 64), halo)] = norm(
            edge.astype(F32), scaling[0, member : member + 1]
        )
        window[member, pl.ds(pl.multiple_of(even * halo, 64), halo)] = normed_own[
            member, pl.ds(pl.multiple_of(odd * (rows - halo), 64), halo)
        ]
        inputs[member, pl.ds(pl.multiple_of(odd * WIN, 32), WIN)] = far[
            pl.ds(pl.multiple_of(member * halo + even * WIN, 32), WIN)
        ]
        inputs[member, pl.ds(pl.multiple_of(even * WIN, 32), WIN)] = latent[
            member, pl.ds(pl.multiple_of(odd * (rows - WIN), 32), WIN)
        ]
        state[member, pl.ds(near_at, rows)] = state_in[member]
        window_next[member, pl.ds(near_at, rows)] = normed_next[member]
    values = layer(
        rows_of(inputs, 0, halo).astype(F32), rows_of(window, WIN, halo), [window[m] for m in range(members)],
        counts, w_in[0], w_out[0], link_count,
    )
    for member in range(members):
        own = values[member * halo : (member + 1) * halo]
        state[member, pl.ds(far_at, halo)] = own
        window_next[member, pl.ds(far_at, halo)] = norm(own, scaling[1, member : member + 1])
    values = layer(
        rows_of(state, WIN, rows), rows_of(window_next, WIN, rows), [window_next[m] for m in range(members)],
        counts_own[...], w_in[1], w_out[1], link_count,
    )
    decoded = dot_nt(w_dec[...], norm(values, dec_gain[...]))
    decoded_out[...] = decoded
    rounded_out[...] = decoded.astype(BF)


def stack_kernel(mine, partner, out):
    wide = mine.shape[1]
    for copy in range(out.shape[0]):
        out[copy, :, :wide] = mine[...]
        out[copy, :, wide:] = partner[...]


def at_grid(parts, incidence):
    channels = parts[0].shape[0]
    fill = -channels % 16
    tail = jnp.zeros((fill, parts[0].shape[1]), BF)
    stacked = jnp.concatenate([piece for part in parts for piece in (part, tail)], axis=0)
    found = dot(stacked, incidence[...])
    step = channels + fill
    return [found[at * step : at * step + channels] for at in range(len(parts))]


def grid_kernel(ensemble, decoded, prior, target, weight, incidence, base_out):
    members = base_out.shape[0]
    nodes = incidence.shape[0]
    own = [part for m in range(members) for part in parts_of(decoded[:, m * nodes : (m + 1) * nodes], 3)]
    at_points = at_grid(own, incidence)
    before = prior[...].astype(F32)
    truth = target[...].astype(F32)
    for member in range(members):
        high, middle, low = at_points[3 * member : 3 * member + 3]
        missed = (before + (low + middle + high)).astype(BF).astype(F32) - truth
        reached = lax.rsqrt(jnp.sum(missed * missed, axis=0, keepdims=True) + DIST_EPS)
        base_out[member] = missed * (reached * weight[...] * (1.0 / ensemble))


def pull_sums(rounded, others, member, members):
    nodes = rounded.shape[1] // members
    step = 128
    pulls = []
    for start in range(member * nodes, (member + 1) * nodes, step):
        anchor = rounded[:, start : start + step].astype(F32)
        total = jnp.zeros_like(anchor)
        for group in range(others.shape[0]):
            for at in range(start % nodes, others.shape[2], nodes):
                offset = anchor - others[group, :, at : at + step].astype(F32)
                near = jnp.sum(offset * offset, axis=0, keepdims=True) + DIST_EPS
                total = total + offset * lax.rsqrt(near)
        pulls.append(total)
    return jnp.concatenate(pulls, axis=1)


def score_kernel(
    ensemble, rounded, others, incidence, base, weight, w_dec, grad_out, vertex_out, grads, vertices, sems
):
    members, channels, _ = base.shape
    nodes = incidence.shape[0]
    factor = weight[...] * (1.0 / (ensemble * (ensemble - 1)))
    copies = []
    pull = [part for m in range(members) for part in parts_of(pull_sums(rounded, others, m, members), 2)]
    at_points = at_grid(pull, incidence)
    for member in range(members):
        high, low = at_points[2 * member : 2 * member + 2]
        grads[member] = (base[member] - factor * (low + high)).astype(BF)
        copies.append(pltpu.make_async_copy(grads.at[member], grad_out.at[member], sems.at[0, member]))
        copies[-1].start()
    for member in range(members):
        high, middle, low = parts_of(dot_nt(incidence[...], grads[member]), 3)
        vertices[member] = (dot(low, w_dec[...]) + dot(middle, w_dec[...]) + dot(high, w_dec[...])).astype(BF)
        copies.append(pltpu.make_async_copy(vertices.at[member], vertex_out.at[member], sems.at[1, member]))
        copies[-1].start()
    for copy in copies:
        copy.wait()


def call(kernel, outs, ins, scratch=(), out_spec=VMEM, weight=0):
    return pl.pallas_call(
        kernel,
        out_shape=[jax.ShapeDtypeStruct(shape, kind) for shape, kind in outs],
        in_specs=ins,
        out_specs=[out_spec] * len(outs),
        scratch_shapes=[pltpu.VMEM(*spec) if isinstance(spec, tuple) else spec for spec in scratch],
        compiler_params=PARAMS,
        cost_estimate=pl.CostEstimate(flops=weight, bytes_accessed=0, transcendentals=0) if weight else None,
    )


def per_device(
    latent, noise_draw, mesh_links, w_cond, w_in, w_out, dec_gain, w_dec,
    target_vertex_map, prior_field, target, location_loss_factor,
):
    members, rows, depth = latent.shape
    channels, points = prior_field.shape
    shards = lax.axis_size("node")
    groups = lax.axis_size("member")
    ensemble = members * groups
    halo = 2 * WIN
    wide = padded(rows + halo)
    sent = (members * halo + 16, depth)
    near_pairs = [(i, i ^ 1) for i in range(shards)]
    far_pairs = [(i, (i + 1) % shards if i % 2 else (i - 1) % shards) for i in range(shards)]

    dma = pltpu.SemaphoreType.DMA

    in_hbm = functools.partial(pltpu.with_memory_space_constraint, memory_space=pltpu.HBM)

    vertex = target_vertex_map.reshape(1, points)
    near, far = call(
        functools.partial(pack_kernel, shards), [(sent, BF)] * 2, [HBM, HBM], [(mesh_links.shape, jnp.int32), dma((1 + 2 * members,))]
    )(in_hbm(latent), in_hbm(mesh_links))
    far = lax.ppermute(far, "node", far_pairs)
    near = lax.ppermute(near, "node", near_pairs)
    state, normed_own, normed_next, counts_own, scaling, incidence = call(
        functools.partial(near_kernel, shards),
        [
            ((members, rows, depth), F32),
            ((members, rows, depth), BF),
            ((members, rows, depth), BF),
            ((rows, wide), BF),
            ((w_cond.shape[0], members, depth), F32),
            ((rows, points), BF),
        ],
        [VMEM] + [HBM] * 7,
        [
            ((members, wide, depth), BF),
            ((members, rows + halo, depth), BF),
            (mesh_links.shape, jnp.int32),
            (noise_draw.shape, F32),
            (w_cond.shape, F32),
            (latent.shape, BF),
            ((1, points), jnp.int32),
            (w_in.shape[1:], BF),
            (w_out.shape[1:], BF),
            dma((7,)),
        ],
    )(near, *map(in_hbm, (mesh_links, noise_draw, w_cond, latent, vertex, w_in, w_out)))
    decoded, rounded = call(
        functools.partial(far_kernel, shards),
        [((channels, members * rows), F32), ((channels, members * rows), BF)],
        [VMEM] * 12,
        [
            ((members, padded(2 * halo), depth), BF),
            ((members, halo, depth), BF),
            ((members, rows + halo, depth), F32),
            ((members, wide, depth), BF),
        ],
    )(
        latent, mesh_links, far, scaling, w_in, w_out, dec_gain.reshape(1, depth), w_dec,
        state, normed_own, normed_next, counts_own,
    )
    partner = lax.ppermute(rounded, "member", [(i, i ^ 1) for i in range(groups)])
    weight = location_loss_factor.reshape(1, points)
    (base,) = call(
        functools.partial(grid_kernel, ensemble), [((members, channels, points), F32)], [VMEM] * 5
    )(decoded, prior_field, target, weight, incidence)
    partner, base = lax.optimization_barrier((partner, base))
    sides = 2
    (stacked,) = call(
        stack_kernel, [((groups // sides, channels, sides * members * rows), BF)], [VMEM] * 2
    )(rounded, partner)
    others = lax.all_to_all(
        stacked, "member", split_axis=0, concat_axis=0, tiled=True,
        axis_index_groups=[list(range(side, groups, sides)) for side in range(sides)],
    )
    return call(
        functools.partial(score_kernel, ensemble),
        [((members, channels, points), BF), ((members, rows, depth), BF)],
        [VMEM] * 6,
        [((members, channels, points), BF), ((members, rows, depth), BF), dma((2, members))],
        HBM,
    )(rounded, others, incidence, base, weight, w_dec)


def solution(mesh):
    in_specs = (
        P("member", "node", None),
        P("member", None),
        P(None, "node"),
        P(),
        P(),
        P(),
        P(),
        P(),
        P("node"),
        P(None, "node"),
        P(None, "node"),
        P("node"),
    )
    out_specs = (P("member", None, "node"), P("member", "node", None))
    return jax.shard_map(
        per_device, mesh=mesh, in_specs=in_specs, out_specs=out_specs, check_vma=False
    )
```

```python
import functools

import jax
import jax.numpy as jnp
from jax import lax
from jax.experimental import pallas as pl
from jax.experimental.pallas import tpu as pltpu
from jax.sharding import PartitionSpec as P

WIN = 96
NORM_EPS = 1e-06
DIST_EPS = 1e-06

LONG = 10**11

BF = jnp.bfloat16
F32 = jnp.float32
VMEM = pl.BlockSpec(memory_space=pltpu.VMEM)
HBM = pl.BlockSpec(memory_space=pltpu.HBM)
PARAMS = pltpu.CompilerParams(vmem_limit_bytes=40 * 2**20)


def dot(lhs, rhs):
    return jnp.dot(lhs, rhs, preferred_element_type=F32)


def dot_nt(lhs, rhs):
    return lax.dot_general(lhs, rhs, (((1,), (1,)), ((), ())), preferred_element_type=F32)


def norm(values, scaling):
    inverse = lax.rsqrt(jnp.mean(values * values, axis=-1, keepdims=True) + NORM_EPS)
    return (values * inverse * scaling).astype(BF)


def silu(values):
    half = 0.5 * values
    return half + half * jnp.tanh(half)


def parts_of(values, count):
    parts = []
    for _ in range(count):
        part = values.astype(BF)
        parts.append(part)
        values = values - part.astype(F32)
    return parts


def padded(rows):
    return -(-rows // 256) * 256


def gains(noise_ref, w_cond_ref, layer):
    return 1.0 + jnp.dot(
        noise_ref[...], w_cond_ref[layer], precision=lax.Precision.HIGHEST, preferred_element_type=F32
    )


def link_offsets(links, first, node_total):
    own = first + lax.broadcasted_iota(jnp.int32, links.shape, 1)
    away = links - own
    away = jnp.where(away > node_total // 2, away - node_total, away)
    away = jnp.where(away < -(node_total // 2), away + node_total, away)
    return away.astype(F32)


def count_matrix(offsets, width):
    link_count, rows = offsets.shape
    places = offsets + (WIN + lax.broadcasted_iota(jnp.int32, offsets.shape, 1)).astype(F32)
    places = jnp.concatenate([places, jnp.full((128 - link_count, rows), -1.0, F32)], axis=0).T
    columns = lax.broadcasted_iota(jnp.int32, (rows, width), 1).astype(F32)
    total = jnp.zeros((rows, width), F32)
    for slot in range(link_count):
        total = total + jnp.where(columns == places[:, slot : slot + 1], 1.0, 0.0)
    return total.astype(BF)


def layer(values, normed, windows, counts, w_in, w_out, link_count):
    rows = values.shape[0] // len(windows)
    sums = [dot(counts, window)[:rows] for window in windows]
    neighbours = (jnp.concatenate(sums, axis=0) * (1.0 / link_count)).astype(BF)
    depth = normed.shape[1]
    preact = dot(normed, w_in[:depth]) + dot(neighbours, w_in[depth:])
    return values + dot(silu(preact).astype(BF), w_out)


def rows_of(array, start, count):
    return jnp.concatenate([array[member, start : start + count] for member in range(array.shape[0])], axis=0)


def position(shards, rows):
    shard = lax.axis_index("node")
    return lax.rem(shard, 2), shard * rows, shards * rows


def fetch_all(pairs, sems):
    fetches = [pltpu.make_async_copy(there, here, sems.at[at]) for at, (there, here) in enumerate(pairs)]
    for fetch in fetches:
        fetch.start()
    return fetches


def pack_kernel(shards, latent, links_in, near, far, links, sems):
    halo = 2 * WIN
    members, rows, _ = latent.shape
    odd, first, node_total = position(shards, rows)
    pairs = [(links_in, links)]
    for send, start in ((near, (1 - odd) * (rows - halo)), (far, odd * (rows - halo))):
        start = pl.multiple_of(start, 64)
        for member in range(members):
            pairs.append((latent.at[member, pl.ds(start, halo)], send.at[pl.ds(member * halo, halo)]))
    fetches = fetch_all(pairs, sems)
    fetches[0].wait()
    offsets = link_offsets(links[...], first, node_total).astype(BF)
    tail = members * halo
    for send in (near, far):
        send[tail:] = jnp.zeros((send.shape[0] - tail, send.shape[1]), BF)
        send[tail : tail + offsets.shape[0], : offsets.shape[1]] = offsets
    for fetch in fetches[1:]:
        fetch.wait()


def received_offsets(received, tail, link_count, rows):
    return received[tail : tail + 16, :rows].astype(F32)[:link_count]


def near_kernel(
    shards, near, links_in, noise_in, w_cond_in, latent_in, vertex_in, w_in_in, w_out_in,
    state_out, normed_own_out, normed_next_out, counts_out, scaling_out, incidence_out, window, inputs,
    links, noise, w_cond, latent, vertex, w_in, w_out, sems
):
    fetches = fetch_all(
        (
            (links_in, links),
            (noise_in, noise),
            (w_cond_in, w_cond),
            (latent_in, latent),
            (vertex_in, vertex),
            (w_in_in.at[0], w_in),
            (w_out_in.at[0], w_out),
        ),
        sems,
    )
    members, rows, _ = latent.shape
    odd, first, node_total = position(shards, rows)
    link_count = links.shape[0]
    halo = 2 * WIN
    own_at = pl.multiple_of(odd * halo, 64)
    near_at = pl.multiple_of((1 - odd) * rows, 64)
    fetches[0].wait()
    own_offsets = link_offsets(links[...], first, node_total)
    near_offsets = received_offsets(near, members * halo, link_count, rows)
    lane = lax.broadcasted_iota(jnp.int32, own_offsets.shape, 1)
    mine = jnp.logical_and(lane >= (1 - odd) * WIN, lane < rows - odd * WIN)
    mixed = jnp.where(mine, own_offsets, near_offsets)
    mixed = pltpu.roll(mixed, rows - WIN - odd * (rows - 2 * WIN), 1)
    counts = count_matrix(mixed, window.shape[1])
    counts_out[...] = count_matrix(own_offsets, window.shape[1])
    for fetch in fetches[1:5]:
        fetch.wait()
    scaling = gains(noise, w_cond, 0)
    next_scaling = gains(noise, w_cond, 1)
    scaling_out[0] = scaling
    scaling_out[1] = next_scaling
    for member in range(members):
        scale = scaling[member : member + 1]
        own = latent[member]
        edge = near[member * halo : (member + 1) * halo]
        inputs[member, pl.ds(own_at, rows)] = own
        inputs[member, pl.ds(near_at, halo)] = edge
        normed_own = norm(own.astype(F32), scale)
        normed_own_out[member] = normed_own
        window[member, rows + halo :] = jnp.zeros((window.shape[1] - rows - halo, window.shape[2]), BF)
        window[member, pl.ds(own_at, rows)] = normed_own
        window[member, pl.ds(near_at, halo)] = norm(edge.astype(F32), scale)
    for fetch in fetches[5:]:
        fetch.wait()
    values = layer(
        rows_of(inputs, WIN, rows).astype(F32), rows_of(window, WIN, rows), [window[m] for m in range(members)],
        counts, w_in[...], w_out[...], link_count,
    )
    for member in range(members):
        own = values[member * rows : (member + 1) * rows]
        state_out[member] = own
        normed_next_out[member] = norm(own, next_scaling[member : member + 1])
    ids = first + lax.broadcasted_iota(jnp.int32, incidence_out.shape, 0)
    incidence_out[...] = jnp.where(ids == vertex[...], 1.0, 0.0).astype(BF)


def far_kernel(
    shards, latent, links, far, scaling, w_in, w_out, dec_gain, w_dec,
    state_in, normed_own, normed_next, counts_own, decoded_out, rounded_out,
    window, inputs, state, window_next,
):
    members, rows, _ = latent.shape
    odd, first, node_total = position(shards, rows)
    even = 1 - odd
    link_count = links.shape[0]
    halo = 2 * WIN
    filled = rows + halo
    own_offsets = link_offsets(links[...], first, node_total)
    far_offsets = received_offsets(far, members * halo, link_count, rows)
    lane = lax.broadcasted_iota(jnp.int32, own_offsets.shape, 1)
    mine = jnp.logical_or(
        jnp.logical_and(odd == 0, lane < WIN), jnp.logical_and(odd == 1, lane >= rows - WIN)
    )
    counts = count_matrix(pltpu.roll(jnp.where(mine, own_offsets, far_offsets), WIN, 1), window.shape[1])
    far_at = pl.multiple_of(odd * rows, 64)
    near_at = pl.multiple_of(even * halo, 64)
    for member in range(members):
        window[member, 2 * halo :] = jnp.zeros((window.shape[1] - 2 * halo, window.shape[2]), BF)
        window_next[member, filled:] = jnp.zeros((window_next.shape[1] - filled, window_next.shape[2]), BF)
        edge = far[member * halo : (member + 1) * halo]
        window[member, pl.ds(pl.multiple_of(odd * halo, 64), halo)] = norm(
            edge.astype(F32), scaling[0, member : member + 1]
        )
        window[member, pl.ds(pl.multiple_of(even * halo, 64), halo)] = normed_own[
            member, pl.ds(pl.multiple_of(odd * (rows - halo), 64), halo)
        ]
        inputs[member, pl.ds(pl.multiple_of(odd * WIN, 32), WIN)] = far[
            pl.ds(pl.multiple_of(member * halo + even * WIN, 32), WIN)
        ]
        inputs[member, pl.ds(pl.multiple_of(even * WIN, 32), WIN)] = latent[
            member, pl.ds(pl.multiple_of(odd * (rows - WIN), 32), WIN)
        ]
        state[member, pl.ds(near_at, rows)] = state_in[member]
        window_next[member, pl.ds(near_at, rows)] = normed_next[member]
    values = layer(
        rows_of(inputs, 0, halo).astype(F32), rows_of(window, WIN, halo), [window[m] for m in range(members)],
        counts, w_in[0], w_out[0], link_count,
    )
    for member in range(members):
        own = values[member * halo : (member + 1) * halo]
        state[member, pl.ds(far_at, halo)] = own
        window_next[member, pl.ds(far_at, halo)] = norm(own, scaling[1, member : member + 1])
    values = layer(
        rows_of(state, WIN, rows), rows_of(window_next, WIN, rows), [window_next[m] for m in range(members)],
        counts_own[...], w_in[1], w_out[1], link_count,
    )
    decoded = dot_nt(w_dec[...], norm(values, dec_gain[...]))
    decoded_out[...] = decoded
    rounded_out[...] = decoded.astype(BF)


def stack_kernel(mine, partner, out):
    wide = mine.shape[1]
    for copy in range(out.shape[0]):
        out[copy, :, :wide] = mine[...]
        out[copy, :, wide:] = partner[...]


def at_grid(parts, incidence):
    channels = parts[0].shape[0]
    fill = -channels % 16
    tail = jnp.zeros((fill, parts[0].shape[1]), BF)
    stacked = jnp.concatenate([piece for part in parts for piece in (part, tail)], axis=0)
    found = dot(stacked, incidence[...])
    step = channels + fill
    return [found[at * step : at * step + channels] for at in range(len(parts))]


def grid_kernel(ensemble, decoded, prior, target, weight, incidence, base_out):
    members = base_out.shape[0]
    nodes = incidence.shape[0]
    own = [part for m in range(members) for part in parts_of(decoded[:, m * nodes : (m + 1) * nodes], 3)]
    at_points = at_grid(own, incidence)
    before = prior[...].astype(F32)
    truth = target[...].astype(F32)
    for member in range(members):
        high, middle, low = at_points[3 * member : 3 * member + 3]
        missed = (before + (low + middle + high)).astype(BF).astype(F32) - truth
        reached = lax.rsqrt(jnp.sum(missed * missed, axis=0, keepdims=True) + DIST_EPS)
        base_out[member] = missed * (reached * weight[...] * (1.0 / ensemble))


def pull_sums(rounded, others, member, members):
    nodes = rounded.shape[1] // members
    step = 128
    pulls = []
    for start in range(member * nodes, (member + 1) * nodes, step):
        anchor = rounded[:, start : start + step].astype(F32)
        total = jnp.zeros_like(anchor)
        for group in range(others.shape[0]):
            for at in range(start % nodes, others.shape[2], nodes):
                offset = anchor - others[group, :, at : at + step].astype(F32)
                near = jnp.sum(offset * offset, axis=0, keepdims=True) + DIST_EPS
                total = total + offset * lax.rsqrt(near)
        pulls.append(total)
    return jnp.concatenate(pulls, axis=1)


def score_kernel(
    ensemble, rounded, others, incidence, base, weight, w_dec, grad_out, vertex_out, grads, both, vertices, sems
):
    members, channels, _ = base.shape
    nodes = incidence.shape[0]
    factor = weight[...] * (1.0 / (ensemble * (ensemble - 1)))
    copies = []
    pull = [part for m in range(members) for part in parts_of(pull_sums(rounded, others, m, members), 2)]
    at_points = at_grid(pull, incidence)
    for member in range(members):
        high, low = at_points[2 * member : 2 * member + 2]
        grads[member] = (base[member] - factor * (low + high)).astype(BF)
    both[...] = jnp.stack([grads[member] for member in range(members)], axis=1)
    copies.append(pltpu.make_async_copy(both, grad_out, sems.at[members]))
    copies[-1].start()
    for member in range(members):
        high, middle, low = parts_of(dot_nt(incidence[...], grads[member]), 3)
        vertices[member] = (dot(low, w_dec[...]) + dot(middle, w_dec[...]) + dot(high, w_dec[...])).astype(BF)
        copies.append(pltpu.make_async_copy(vertices.at[member], vertex_out.at[member], sems.at[member]))
        copies[-1].start()
    for copy in copies:
        copy.wait()


def call(kernel, outs, ins, scratch=(), out_spec=VMEM, weight=0):
    return pl.pallas_call(
        kernel,
        out_shape=[jax.ShapeDtypeStruct(shape, kind) for shape, kind in outs],
        in_specs=ins,
        out_specs=[out_spec] * len(outs),
        scratch_shapes=[pltpu.VMEM(*spec) if isinstance(spec, tuple) else spec for spec in scratch],
        compiler_params=PARAMS,
        cost_estimate=pl.CostEstimate(flops=weight, bytes_accessed=0, transcendentals=0) if weight else None,
    )


def per_device(
    latent, noise_draw, mesh_links, w_cond, w_in, w_out, dec_gain, w_dec,
    target_vertex_map, prior_field, target, location_loss_factor,
):
    members, rows, depth = latent.shape
    channels, points = prior_field.shape
    shards = lax.axis_size("node")
    groups = lax.axis_size("member")
    ensemble = members * groups
    halo = 2 * WIN
    wide = padded(rows + halo)
    sent = (members * halo + 16, depth)
    near_pairs = [(i, i ^ 1) for i in range(shards)]
    far_pairs = [(i, (i + 1) % shards if i % 2 else (i - 1) % shards) for i in range(shards)]

    dma = pltpu.SemaphoreType.DMA

    in_hbm = functools.partial(pltpu.with_memory_space_constraint, memory_space=pltpu.HBM)

    vertex = target_vertex_map.reshape(1, points)
    near, far = call(
        functools.partial(pack_kernel, shards), [(sent, BF)] * 2, [HBM, HBM], [(mesh_links.shape, jnp.int32), dma((1 + 2 * members,))]
    )(in_hbm(latent), in_hbm(mesh_links))
    far = lax.ppermute(far, "node", far_pairs)
    near = lax.ppermute(near, "node", near_pairs)
    state, normed_own, normed_next, counts_own, scaling, incidence = call(
        functools.partial(near_kernel, shards),
        [
            ((members, rows, depth), F32),
            ((members, rows, depth), BF),
            ((members, rows, depth), BF),
            ((rows, wide), BF),
            ((w_cond.shape[0], members, depth), F32),
            ((rows, points), BF),
        ],
        [VMEM] + [HBM] * 7,
        [
            ((members, wide, depth), BF),
            ((members, rows + halo, depth), BF),
            (mesh_links.shape, jnp.int32),
            (noise_draw.shape, F32),
            (w_cond.shape, F32),
            (latent.shape, BF),
            ((1, points), jnp.int32),
            (w_in.shape[1:], BF),
            (w_out.shape[1:], BF),
            dma((7,)),
        ],
    )(near, *map(in_hbm, (mesh_links, noise_draw, w_cond, latent, vertex, w_in, w_out)))
    decoded, rounded = call(
        functools.partial(far_kernel, shards),
        [((channels, members * rows), F32), ((channels, members * rows), BF)],
        [VMEM] * 12,
        [
            ((members, padded(2 * halo), depth), BF),
            ((members, halo, depth), BF),
            ((members, rows + halo, depth), F32),
            ((members, wide, depth), BF),
        ],
    )(
        latent, mesh_links, far, scaling, w_in, w_out, dec_gain.reshape(1, depth), w_dec,
        state, normed_own, normed_next, counts_own,
    )
    partner = lax.ppermute(rounded, "member", [(i, i ^ 1) for i in range(groups)])
    weight = location_loss_factor.reshape(1, points)
    (base,) = call(
        functools.partial(grid_kernel, ensemble), [((members, channels, points), F32)], [VMEM] * 5
    )(decoded, prior_field, target, weight, incidence)
    partner, base = lax.optimization_barrier((partner, base))
    sides = 2
    (stacked,) = call(
        stack_kernel, [((groups // sides, channels, sides * members * rows), BF)], [VMEM] * 2
    )(rounded, partner)
    others = lax.all_to_all(
        stacked, "member", split_axis=0, concat_axis=0, tiled=True,
        axis_index_groups=[list(range(side, groups, sides)) for side in range(sides)],
    )
    grads, vertices = call(
        functools.partial(score_kernel, ensemble),
        [((channels, members, points), BF), ((members, rows, depth), BF)],
        [VMEM] * 6,
        [
            ((members, channels, points), BF),
            ((channels, members, points), BF),
            ((members, rows, depth), BF),
            dma((members + 1,)),
        ],
        HBM,
    )(rounded, others, incidence, base, weight, w_dec)
    return jnp.transpose(grads, (1, 0, 2)), vertices


def solution(mesh):
    in_specs = (
        P("member", "node", None),
        P("member", None),
        P(None, "node"),
        P(),
        P(),
        P(),
        P(),
        P(),
        P("node"),
        P(None, "node"),
        P(None, "node"),
        P("node"),
    )
    out_specs = (P("member", None, "node"), P("member", "node", None))
    return jax.shard_map(
        per_device, mesh=mesh, in_specs=in_specs, out_specs=out_specs, check_vma=False
    )
```

```python
import functools

import jax
import jax.numpy as jnp
from jax import lax
from jax.experimental import pallas as pl
from jax.experimental.pallas import tpu as pltpu
from jax.sharding import PartitionSpec as P

WIN = 96
NORM_EPS = 1e-06
DIST_EPS = 1e-06

LONG = 10**11

BF = jnp.bfloat16
F32 = jnp.float32
VMEM = pl.BlockSpec(memory_space=pltpu.VMEM)
HBM = pl.BlockSpec(memory_space=pltpu.HBM)
PARAMS = pltpu.CompilerParams(vmem_limit_bytes=40 * 2**20)


def dot(lhs, rhs):
    return jnp.dot(lhs, rhs, preferred_element_type=F32)


def dot_nt(lhs, rhs):
    return lax.dot_general(lhs, rhs, (((1,), (1,)), ((), ())), preferred_element_type=F32)


def norm(values, scaling):
    inverse = lax.rsqrt(jnp.mean(values * values, axis=-1, keepdims=True) + NORM_EPS)
    return (values * inverse * scaling).astype(BF)


def silu(values):
    half = 0.5 * values
    return half + half * jnp.tanh(half)


def parts_of(values, count):
    parts = []
    for _ in range(count):
        part = values.astype(BF)
        parts.append(part)
        values = values - part.astype(F32)
    return parts


def padded(rows):
    return -(-rows // 256) * 256


def gains(noise_ref, w_cond_ref, layer):
    return 1.0 + jnp.dot(
        noise_ref[...], w_cond_ref[layer], precision=lax.Precision.HIGHEST, preferred_element_type=F32
    )


def link_offsets(links, first, node_total):
    own = first + lax.broadcasted_iota(jnp.int32, links.shape, 1)
    away = links - own
    away = jnp.where(away > node_total // 2, away - node_total, away)
    away = jnp.where(away < -(node_total // 2), away + node_total, away)
    return away.astype(F32)


def count_matrix(offsets, width):
    link_count, rows = offsets.shape
    places = offsets + (WIN + lax.broadcasted_iota(jnp.int32, offsets.shape, 1)).astype(F32)
    places = jnp.concatenate([places, jnp.full((128 - link_count, rows), -1.0, F32)], axis=0).T
    columns = lax.broadcasted_iota(jnp.int32, (rows, width), 1).astype(F32)
    total = jnp.zeros((rows, width), F32)
    for slot in range(link_count):
        total = total + jnp.where(columns == places[:, slot : slot + 1], 1.0, 0.0)
    return total.astype(BF)


def layer(values, normed, windows, counts, w_in, w_out, link_count):
    rows = values.shape[0] // len(windows)
    sums = [dot(counts, window)[:rows] for window in windows]
    neighbours = (jnp.concatenate(sums, axis=0) * (1.0 / link_count)).astype(BF)
    depth = normed.shape[1]
    preact = dot(normed, w_in[:depth]) + dot(neighbours, w_in[depth:])
    return values + dot(silu(preact).astype(BF), w_out)


def rows_of(array, start, count):
    return jnp.concatenate([array[member, start : start + count] for member in range(array.shape[0])], axis=0)


def position(shards, rows):
    shard = lax.axis_index("node")
    return lax.rem(shard, 2), shard * rows, shards * rows


def fetch_all(pairs, sems):
    fetches = [pltpu.make_async_copy(there, here, sems.at[at]) for at, (there, here) in enumerate(pairs)]
    for fetch in fetches:
        fetch.start()
    return fetches


def pack_kernel(shards, latent, links_in, near, far, links, sems):
    halo = 2 * WIN
    members, rows, _ = latent.shape
    odd, first, node_total = position(shards, rows)
    pairs = [(links_in, links)]
    for send, start in ((near, (1 - odd) * (rows - halo)), (far, odd * (rows - halo))):
        start = pl.multiple_of(start, 64)
        for member in range(members):
            pairs.append((latent.at[member, pl.ds(start, halo)], send.at[pl.ds(member * halo, halo)]))
    fetches = fetch_all(pairs, sems)
    fetches[0].wait()
    offsets = link_offsets(links[...], first, node_total).astype(BF)
    tail = members * halo
    for send in (near, far):
        send[tail:] = jnp.zeros((send.shape[0] - tail, send.shape[1]), BF)
        send[tail : tail + offsets.shape[0], : offsets.shape[1]] = offsets
    for fetch in fetches[1:]:
        fetch.wait()


def received_offsets(received, tail, link_count, rows):
    return received[tail : tail + 16, :rows].astype(F32)[:link_count]


def near_kernel(
    shards, near, links_in, noise_in, w_cond_in, latent_in, vertex_in, w_in_in, w_out_in,
    state_out, normed_own_out, normed_next_out, counts_out, scaling_out, incidence_out, window, inputs,
    links, noise, w_cond, latent, vertex, w_in, w_out, sems
):
    fetches = fetch_all(
        (
            (links_in, links),
            (noise_in, noise),
            (w_cond_in, w_cond),
            (latent_in, latent),
            (vertex_in, vertex),
            (w_in_in.at[0], w_in),
            (w_out_in.at[0], w_out),
        ),
        sems,
    )
    members, rows, _ = latent.shape
    odd, first, node_total = position(shards, rows)
    link_count = links.shape[0]
    halo = 2 * WIN
    own_at = pl.multiple_of(odd * halo, 64)
    near_at = pl.multiple_of((1 - odd) * rows, 64)
    fetches[0].wait()
    own_offsets = link_offsets(links[...], first, node_total)
    near_offsets = received_offsets(near, members * halo, link_count, rows)
    lane = lax.broadcasted_iota(jnp.int32, own_offsets.shape, 1)
    mine = jnp.logical_and(lane >= (1 - odd) * WIN, lane < rows - odd * WIN)
    mixed = jnp.where(mine, own_offsets, near_offsets)
    mixed = pltpu.roll(mixed, rows - WIN - odd * (rows - 2 * WIN), 1)
    counts = count_matrix(mixed, window.shape[1])
    counts_out[...] = count_matrix(own_offsets, window.shape[1])
    for fetch in fetches[1:5]:
        fetch.wait()
    scaling = gains(noise, w_cond, 0)
    next_scaling = gains(noise, w_cond, 1)
    scaling_out[0] = scaling
    scaling_out[1] = next_scaling
    for member in range(members):
        scale = scaling[member : member + 1]
        own = latent[member]
        edge = near[member * halo : (member + 1) * halo]
        inputs[member, pl.ds(own_at, rows)] = own
        inputs[member, pl.ds(near_at, halo)] = edge
        normed_own = norm(own.astype(F32), scale)
        normed_own_out[member] = normed_own
        window[member, rows + halo :] = jnp.zeros((window.shape[1] - rows - halo, window.shape[2]), BF)
        window[member, pl.ds(own_at, rows)] = normed_own
        window[member, pl.ds(near_at, halo)] = norm(edge.astype(F32), scale)
    for fetch in fetches[5:]:
        fetch.wait()
    values = layer(
        rows_of(inputs, WIN, rows).astype(F32), rows_of(window, WIN, rows), [window[m] for m in range(members)],
        counts, w_in[...], w_out[...], link_count,
    )
    for member in range(members):
        own = values[member * rows : (member + 1) * rows]
        state_out[member] = own
        normed_next_out[member] = norm(own, next_scaling[member : member + 1])
    ids = first + lax.broadcasted_iota(jnp.int32, incidence_out.shape, 0)
    incidence_out[...] = jnp.where(ids == vertex[...], 1.0, 0.0).astype(BF)


def far_kernel(
    shards, latent, links, far, scaling, w_in, w_out, dec_gain, w_dec,
    state_in, normed_own, normed_next, counts_own, decoded_out, rounded_out,
    window, inputs, state, window_next,
):
    members, rows, _ = latent.shape
    odd, first, node_total = position(shards, rows)
    even = 1 - odd
    link_count = links.shape[0]
    halo = 2 * WIN
    filled = rows + halo
    own_offsets = link_offsets(links[...], first, node_total)
    far_offsets = received_offsets(far, members * halo, link_count, rows)
    lane = lax.broadcasted_iota(jnp.int32, own_offsets.shape, 1)
    mine = jnp.logical_or(
        jnp.logical_and(odd == 0, lane < WIN), jnp.logical_and(odd == 1, lane >= rows - WIN)
    )
    counts = count_matrix(pltpu.roll(jnp.where(mine, own_offsets, far_offsets), WIN, 1), window.shape[1])
    far_at = pl.multiple_of(odd * rows, 64)
    near_at = pl.multiple_of(even * halo, 64)
    for member in range(members):
        window_next[member, filled:] = jnp.zeros((window_next.shape[1] - filled, window_next.shape[2]), BF)
        edge = far[member * halo : (member + 1) * halo]
        window[member, pl.ds(pl.multiple_of(odd * halo, 64), halo)] = norm(
            edge.astype(F32), scaling[0, member : member + 1]
        )
        window[member, pl.ds(pl.multiple_of(even * halo, 64), halo)] = normed_own[
            member, pl.ds(pl.multiple_of(odd * (rows - halo), 64), halo)
        ]
        inputs[member, pl.ds(pl.multiple_of(odd * WIN, 32), WIN)] = far[
            pl.ds(pl.multiple_of(member * halo + even * WIN, 32), WIN)
        ]
        inputs[member, pl.ds(pl.multiple_of(even * WIN, 32), WIN)] = latent[
            member, pl.ds(pl.multiple_of(odd * (rows - WIN), 32), WIN)
        ]
        state[member, pl.ds(near_at, rows)] = state_in[member]
        window_next[member, pl.ds(near_at, rows)] = normed_next[member]
    values = layer(
        rows_of(inputs, 0, halo).astype(F32), rows_of(window, WIN, halo), [window[m] for m in range(members)],
        counts, w_in[0], w_out[0], link_count,
    )
    for member in range(members):
        own = values[member * halo : (member + 1) * halo]
        state[member, pl.ds(far_at, halo)] = own
        window_next[member, pl.ds(far_at, halo)] = norm(own, scaling[1, member : member + 1])
    values = layer(
        rows_of(state, WIN, rows), rows_of(window_next, WIN, rows), [window_next[m] for m in range(members)],
        counts_own[...], w_in[1], w_out[1], link_count,
    )
    decoded = dot_nt(w_dec[...], norm(values, dec_gain[...]))
    decoded_out[...] = decoded
    rounded_out[...] = decoded.astype(BF)


def stack_kernel(mine, partner, out):
    wide = mine.shape[1]
    for copy in range(out.shape[0]):
        out[copy, :, :wide] = mine[...]
        out[copy, :, wide:] = partner[...]


def at_grid(parts, incidence):
    channels = parts[0].shape[0]
    fill = -channels % 16
    tail = jnp.zeros((fill, parts[0].shape[1]), BF)
    stacked = jnp.concatenate([piece for part in parts for piece in (part, tail)], axis=0)
    found = dot(stacked, incidence[...])
    step = channels + fill
    return [found[at * step : at * step + channels] for at in range(len(parts))]


def grid_kernel(ensemble, decoded, prior, target, weight, incidence, base_out):
    members = base_out.shape[0]
    nodes = incidence.shape[0]
    own = [part for m in range(members) for part in parts_of(decoded[:, m * nodes : (m + 1) * nodes], 3)]
    at_points = at_grid(own, incidence)
    before = prior[...].astype(F32)
    truth = target[...].astype(F32)
    for member in range(members):
        high, middle, low = at_points[3 * member : 3 * member + 3]
        missed = (before + (low + middle + high)).astype(BF).astype(F32) - truth
        reached = lax.rsqrt(jnp.sum(missed * missed, axis=0, keepdims=True) + DIST_EPS)
        base_out[member] = missed * (reached * weight[...] * (1.0 / ensemble))


def pull_sums(rounded, others, member, members):
    nodes = rounded.shape[1] // members
    step = 128
    pulls = []
    for start in range(member * nodes, (member + 1) * nodes, step):
        anchor = rounded[:, start : start + step].astype(F32)
        total = jnp.zeros_like(anchor)
        for group in range(others.shape[0]):
            for at in range(start % nodes, others.shape[2], nodes):
                offset = anchor - others[group, :, at : at + step].astype(F32)
                near = jnp.sum(offset * offset, axis=0, keepdims=True) + DIST_EPS
                total = total + offset * lax.rsqrt(near)
        pulls.append(total)
    return jnp.concatenate(pulls, axis=1)


def score_kernel(
    ensemble, rounded, others, incidence, base, weight, w_dec, grad_out, vertex_out, grads, both, vertices, sems
):
    members, channels, _ = base.shape
    nodes = incidence.shape[0]
    lanes = grads.shape[1]
    factor = weight[...] * (1.0 / (ensemble * (ensemble - 1)))
    copies = []
    pull = [part for m in range(members) for part in parts_of(pull_sums(rounded, others, m, members), 2)]
    at_points = at_grid(pull, incidence)
    for member in range(members):
        high, low = at_points[2 * member : 2 * member + 2]
        grad = (base[member] - factor * (low + high)).astype(BF)
        grads[member] = jnp.concatenate([grad, jnp.zeros((lanes - channels, grad.shape[1]), BF)], axis=0)
    both[...] = jnp.stack([grads[member, :channels] for member in range(members)], axis=1)
    copies.append(pltpu.make_async_copy(both, grad_out, sems.at[members]))
    copies[-1].start()
    by_node = dot_nt(incidence[...], jnp.concatenate([grads[member] for member in range(members)], axis=0))
    filled = jnp.concatenate([w_dec[...], jnp.zeros((lanes - channels, w_dec.shape[1]), BF)], axis=0)
    weights = jnp.concatenate([filled, filled], axis=0)
    for member in range(members):
        parts = parts_of(by_node[:, member * lanes : (member + 1) * lanes], 2)
        vertices[member] = dot(jnp.concatenate(parts, axis=1), weights).astype(BF)
        copies.append(pltpu.make_async_copy(vertices.at[member], vertex_out.at[member], sems.at[member]))
        copies[-1].start()
    for copy in copies:
        copy.wait()


def call(kernel, outs, ins, scratch=(), out_spec=VMEM, weight=0):
    return pl.pallas_call(
        kernel,
        out_shape=[jax.ShapeDtypeStruct(shape, kind) for shape, kind in outs],
        in_specs=ins,
        out_specs=[out_spec] * len(outs),
        scratch_shapes=[pltpu.VMEM(*spec) if isinstance(spec, tuple) else spec for spec in scratch],
        compiler_params=PARAMS,
        cost_estimate=pl.CostEstimate(flops=weight, bytes_accessed=0, transcendentals=0) if weight else None,
    )


def per_device(
    latent, noise_draw, mesh_links, w_cond, w_in, w_out, dec_gain, w_dec,
    target_vertex_map, prior_field, target, location_loss_factor,
):
    members, rows, depth = latent.shape
    channels, points = prior_field.shape
    shards = lax.axis_size("node")
    groups = lax.axis_size("member")
    ensemble = members * groups
    halo = 2 * WIN
    wide = padded(rows + halo)
    sent = (members * halo + 16, depth)
    near_pairs = [(i, i ^ 1) for i in range(shards)]
    far_pairs = [(i, (i + 1) % shards if i % 2 else (i - 1) % shards) for i in range(shards)]

    dma = pltpu.SemaphoreType.DMA

    in_hbm = functools.partial(pltpu.with_memory_space_constraint, memory_space=pltpu.HBM)

    vertex = target_vertex_map.reshape(1, points)
    near, far = call(
        functools.partial(pack_kernel, shards), [(sent, BF)] * 2, [HBM, HBM], [(mesh_links.shape, jnp.int32), dma((1 + 2 * members,))]
    )(in_hbm(latent), in_hbm(mesh_links))
    far = lax.ppermute(far, "node", far_pairs)
    near = lax.ppermute(near, "node", near_pairs)
    state, normed_own, normed_next, counts_own, scaling, incidence = call(
        functools.partial(near_kernel, shards),
        [
            ((members, rows, depth), F32),
            ((members, rows, depth), BF),
            ((members, rows, depth), BF),
            ((rows, wide), BF),
            ((w_cond.shape[0], members, depth), F32),
            ((rows, points), BF),
        ],
        [VMEM] + [HBM] * 7,
        [
            ((members, wide, depth), BF),
            ((members, rows + halo, depth), BF),
            (mesh_links.shape, jnp.int32),
            (noise_draw.shape, F32),
            (w_cond.shape, F32),
            (latent.shape, BF),
            ((1, points), jnp.int32),
            (w_in.shape[1:], BF),
            (w_out.shape[1:], BF),
            dma((7,)),
        ],
    )(near, *map(in_hbm, (mesh_links, noise_draw, w_cond, latent, vertex, w_in, w_out)))
    decoded, rounded = call(
        functools.partial(far_kernel, shards),
        [((channels, members * rows), F32), ((channels, members * rows), BF)],
        [VMEM] * 12,
        [
            ((members, 2 * halo, depth), BF),
            ((members, halo, depth), BF),
            ((members, rows + halo, depth), F32),
            ((members, wide, depth), BF),
        ],
    )(
        latent, mesh_links, far, scaling, w_in, w_out, dec_gain.reshape(1, depth), w_dec,
        state, normed_own, normed_next, counts_own,
    )
    partner = lax.ppermute(rounded, "member", [(i, i ^ 1) for i in range(groups)])
    weight = location_loss_factor.reshape(1, points)
    (base,) = call(
        functools.partial(grid_kernel, ensemble), [((members, channels, points), F32)], [VMEM] * 5
    )(decoded, prior_field, target, weight, incidence)
    partner, base = lax.optimization_barrier((partner, base))
    sides = 2
    (stacked,) = call(
        stack_kernel, [((groups // sides, channels, sides * members * rows), BF)], [VMEM] * 2
    )(rounded, partner)
    others = lax.all_to_all(
        stacked, "member", split_axis=0, concat_axis=0, tiled=True,
        axis_index_groups=[list(range(side, groups, sides)) for side in range(sides)],
    )
    grads, vertices = call(
        functools.partial(score_kernel, ensemble),
        [((channels, members, points), BF), ((members, rows, depth), BF)],
        [VMEM] * 6,
        [
            ((members, channels + -channels % 128, points), BF),
            ((channels, members, points), BF),
            ((members, rows, depth), BF),
            dma((members + 1,)),
        ],
        HBM,
    )(rounded, others, incidence, base, weight, w_dec)
    return jnp.transpose(grads, (1, 0, 2)), vertices


def solution(mesh):
    in_specs = (
        P("member", "node", None),
        P("member", None),
        P(None, "node"),
        P(),
        P(),
        P(),
        P(),
        P(),
        P("node"),
        P(None, "node"),
        P(None, "node"),
        P("node"),
    )
    out_specs = (P("member", None, "node"), P("member", "node", None))
    return jax.shard_map(
        per_device, mesh=mesh, in_specs=in_specs, out_specs=out_specs, check_vma=False
    )
```

```python
import functools

import jax
import jax.numpy as jnp
from jax import lax
from jax.experimental import pallas as pl
from jax.experimental.pallas import tpu as pltpu
from jax.sharding import PartitionSpec as P

WIN = 96
NORM_EPS = 1e-06
DIST_EPS = 1e-06

LONG = 10**11

BF = jnp.bfloat16
F32 = jnp.float32
VMEM = pl.BlockSpec(memory_space=pltpu.VMEM)
HBM = pl.BlockSpec(memory_space=pltpu.HBM)
PARAMS = pltpu.CompilerParams(vmem_limit_bytes=40 * 2**20)


def dot(lhs, rhs):
    return jnp.dot(lhs, rhs, preferred_element_type=F32)


def dot_nt(lhs, rhs):
    return lax.dot_general(lhs, rhs, (((1,), (1,)), ((), ())), preferred_element_type=F32)


def norm(values, scaling):
    inverse = lax.rsqrt(jnp.mean(values * values, axis=-1, keepdims=True) + NORM_EPS)
    return (values * inverse * scaling).astype(BF)


def silu(values):
    half = 0.5 * values
    return half + half * jnp.tanh(half)


def parts_of(values, count):
    parts = []
    for _ in range(count):
        part = values.astype(BF)
        parts.append(part)
        values = values - part.astype(F32)
    return parts


def padded(rows):
    return -(-rows // 256) * 256


def gains(noise_ref, w_cond_ref, layer):
    return 1.0 + jnp.dot(
        noise_ref[...], w_cond_ref[layer], precision=lax.Precision.HIGHEST, preferred_element_type=F32
    )


def link_offsets(links, first, node_total):
    own = first + lax.broadcasted_iota(jnp.int32, links.shape, 1)
    away = links - own
    away = jnp.where(away > node_total // 2, away - node_total, away)
    away = jnp.where(away < -(node_total // 2), away + node_total, away)
    return away.astype(F32)


def count_matrix(offsets, width):
    link_count, rows = offsets.shape
    places = offsets + (WIN + lax.broadcasted_iota(jnp.int32, offsets.shape, 1)).astype(F32)
    places = jnp.concatenate([places, jnp.full((128 - link_count, rows), -1.0, F32)], axis=0).T
    columns = lax.broadcasted_iota(jnp.int32, (rows, width), 1).astype(F32)
    total = jnp.zeros((rows, width), F32)
    for slot in range(link_count):
        total = total + jnp.where(columns == places[:, slot : slot + 1], 1.0, 0.0)
    return total.astype(BF)


def layer(values, normed, windows, counts, w_in, w_out, link_count):
    rows = values.shape[0] // len(windows)
    sums = [dot(counts, window)[:rows] for window in windows]
    neighbours = (jnp.concatenate(sums, axis=0) * (1.0 / link_count)).astype(BF)
    preact = dot(jnp.concatenate([normed, neighbours], axis=1), w_in[...])
    return values + dot(silu(preact).astype(BF), w_out)


def rows_of(array, start, count):
    return jnp.concatenate([array[member, start : start + count] for member in range(array.shape[0])], axis=0)


def position(shards, rows):
    shard = lax.axis_index("node")
    return lax.rem(shard, 2), shard * rows, shards * rows


def fetch_all(pairs, sems):
    fetches = [pltpu.make_async_copy(there, here, sems.at[at]) for at, (there, here) in enumerate(pairs)]
    for fetch in fetches:
        fetch.start()
    return fetches


def pack_kernel(shards, latent, links_in, near, far, links, sems):
    halo = 2 * WIN
    members, rows, _ = latent.shape
    odd, first, node_total = position(shards, rows)
    pairs = [(links_in, links)]
    for send, start in ((near, (1 - odd) * (rows - halo)), (far, odd * (rows - halo))):
        start = pl.multiple_of(start, 64)
        for member in range(members):
            pairs.append((latent.at[member, pl.ds(start, halo)], send.at[pl.ds(member * halo, halo)]))
    fetches = fetch_all(pairs, sems)
    fetches[0].wait()
    offsets = link_offsets(links[...], first, node_total).astype(BF)
    tail = members * halo
    for send in (near, far):
        send[tail:] = jnp.zeros((send.shape[0] - tail, send.shape[1]), BF)
        send[tail : tail + offsets.shape[0], : offsets.shape[1]] = offsets
    for fetch in fetches[1:]:
        fetch.wait()


def received_offsets(received, tail, link_count, rows):
    return received[tail : tail + 16, :rows].astype(F32)[:link_count]


def near_kernel(
    shards, near, links_in, noise_in, w_cond_in, latent_in, vertex_in, w_in_in, w_out_in,
    state_out, normed_own_out, normed_next_out, counts_out, scaling_out, incidence_out, window, inputs,
    links, noise, w_cond, latent, vertex, w_in, w_out, sems
):
    fetches = fetch_all(
        (
            (links_in, links),
            (noise_in, noise),
            (w_cond_in, w_cond),
            (latent_in, latent),
            (vertex_in, vertex),
            (w_in_in.at[0], w_in),
            (w_out_in.at[0], w_out),
        ),
        sems,
    )
    members, rows, _ = latent.shape
    odd, first, node_total = position(shards, rows)
    link_count = links.shape[0]
    halo = 2 * WIN
    own_at = pl.multiple_of(odd * halo, 64)
    near_at = pl.multiple_of((1 - odd) * rows, 64)
    fetches[0].wait()
    own_offsets = link_offsets(links[...], first, node_total)
    near_offsets = received_offsets(near, members * halo, link_count, rows)
    lane = lax.broadcasted_iota(jnp.int32, own_offsets.shape, 1)
    mine = jnp.logical_and(lane >= (1 - odd) * WIN, lane < rows - odd * WIN)
    mixed = jnp.where(mine, own_offsets, near_offsets)
    mixed = pltpu.roll(mixed, rows - WIN - odd * (rows - 2 * WIN), 1)
    counts = count_matrix(mixed, window.shape[1])
    counts_out[...] = count_matrix(own_offsets, window.shape[1])
    for fetch in fetches[1:5]:
        fetch.wait()
    scaling = gains(noise, w_cond, 0)
    next_scaling = gains(noise, w_cond, 1)
    scaling_out[0] = scaling
    scaling_out[1] = next_scaling
    for member in range(members):
        scale = scaling[member : member + 1]
        own = latent[member]
        edge = near[member * halo : (member + 1) * halo]
        inputs[member, pl.ds(own_at, rows)] = own
        inputs[member, pl.ds(near_at, halo)] = edge
        normed_own = norm(own.astype(F32), scale)
        normed_own_out[member] = normed_own
        window[member, rows + halo :] = jnp.zeros((window.shape[1] - rows - halo, window.shape[2]), BF)
        window[member, pl.ds(own_at, rows)] = normed_own
        window[member, pl.ds(near_at, halo)] = norm(edge.astype(F32), scale)
    for fetch in fetches[5:]:
        fetch.wait()
    values = layer(
        rows_of(inputs, WIN, rows).astype(F32), rows_of(window, WIN, rows), [window[m] for m in range(members)],
        counts, w_in, w_out[...], link_count,
    )
    for member in range(members):
        own = values[member * rows : (member + 1) * rows]
        state_out[member] = own
        normed_next_out[member] = norm(own, next_scaling[member : member + 1])
    ids = first + lax.broadcasted_iota(jnp.int32, incidence_out.shape, 0)
    incidence_out[...] = jnp.where(ids == vertex[...], 1.0, 0.0).astype(BF)


def far_kernel(
    shards, latent, links, far, scaling, w_in, w_out, dec_gain, w_dec,
    state_in, normed_own, normed_next, counts_own, decoded_out, rounded_out,
    window, inputs, state, window_next,
):
    members, rows, _ = latent.shape
    odd, first, node_total = position(shards, rows)
    even = 1 - odd
    link_count = links.shape[0]
    halo = 2 * WIN
    filled = rows + halo
    own_offsets = link_offsets(links[...], first, node_total)
    far_offsets = received_offsets(far, members * halo, link_count, rows)
    lane = lax.broadcasted_iota(jnp.int32, own_offsets.shape, 1)
    mine = jnp.logical_or(
        jnp.logical_and(odd == 0, lane < WIN), jnp.logical_and(odd == 1, lane >= rows - WIN)
    )
    counts = count_matrix(pltpu.roll(jnp.where(mine, own_offsets, far_offsets), WIN, 1), window.shape[1])
    far_at = pl.multiple_of(odd * rows, 64)
    near_at = pl.multiple_of(even * halo, 64)
    for member in range(members):
        window_next[member, filled:] = jnp.zeros((window_next.shape[1] - filled, window_next.shape[2]), BF)
        edge = far[member * halo : (member + 1) * halo]
        window[member, pl.ds(pl.multiple_of(odd * halo, 64), halo)] = norm(
            edge.astype(F32), scaling[0, member : member + 1]
        )
        window[member, pl.ds(pl.multiple_of(even * halo, 64), halo)] = normed_own[
            member, pl.ds(pl.multiple_of(odd * (rows - halo), 64), halo)
        ]
        inputs[member, pl.ds(pl.multiple_of(odd * WIN, 32), WIN)] = far[
            pl.ds(pl.multiple_of(member * halo + even * WIN, 32), WIN)
        ]
        inputs[member, pl.ds(pl.multiple_of(even * WIN, 32), WIN)] = latent[
            member, pl.ds(pl.multiple_of(odd * (rows - WIN), 32), WIN)
        ]
        state[member, pl.ds(near_at, rows)] = state_in[member]
        window_next[member, pl.ds(near_at, rows)] = normed_next[member]
    values = layer(
        rows_of(inputs, 0, halo).astype(F32), rows_of(window, WIN, halo), [window[m] for m in range(members)],
        counts, w_in.at[0], w_out[0], link_count,
    )
    for member in range(members):
        own = values[member * halo : (member + 1) * halo]
        state[member, pl.ds(far_at, halo)] = own
        window_next[member, pl.ds(far_at, halo)] = norm(own, scaling[1, member : member + 1])
    values = layer(
        rows_of(state, WIN, rows), rows_of(window_next, WIN, rows), [window_next[m] for m in range(members)],
        counts_own[...], w_in.at[1], w_out[1], link_count,
    )
    decoded = dot_nt(w_dec[...], norm(values, dec_gain[...]))
    decoded_out[...] = decoded
    rounded_out[...] = decoded.astype(BF)


def stack_kernel(mine, partner, out):
    wide = mine.shape[1]
    for copy in range(out.shape[0]):
        out[copy, :, :wide] = mine[...]
        out[copy, :, wide:] = partner[...]


def at_grid(parts, incidence):
    channels = parts[0].shape[0]
    fill = -channels % 16
    tail = jnp.zeros((fill, parts[0].shape[1]), BF)
    stacked = jnp.concatenate([piece for part in parts for piece in (part, tail)], axis=0)
    found = dot(stacked, incidence[...])
    step = channels + fill
    return [found[at * step : at * step + channels] for at in range(len(parts))]


def grid_kernel(ensemble, decoded, prior, target, weight, incidence, base_out):
    members = base_out.shape[0]
    nodes = incidence.shape[0]
    own = [part for m in range(members) for part in parts_of(decoded[:, m * nodes : (m + 1) * nodes], 3)]
    at_points = at_grid(own, incidence)
    before = prior[...].astype(F32)
    truth = target[...].astype(F32)
    for member in range(members):
        high, middle, low = at_points[3 * member : 3 * member + 3]
        missed = (before + (low + middle + high)).astype(BF).astype(F32) - truth
        reached = lax.rsqrt(jnp.sum(missed * missed, axis=0, keepdims=True) + DIST_EPS)
        base_out[member] = missed * (reached * weight[...] * (1.0 / ensemble))


def pull_sums(rounded, others, member, members):
    nodes = rounded.shape[1] // members
    step = 128
    pulls = []
    for start in range(member * nodes, (member + 1) * nodes, step):
        anchor = rounded[:, start : start + step].astype(F32)
        total = jnp.zeros_like(anchor)
        for group in range(others.shape[0]):
            for at in range(start % nodes, others.shape[2], nodes):
                offset = anchor - others[group, :, at : at + step].astype(F32)
                near = jnp.sum(offset * offset, axis=0, keepdims=True) + DIST_EPS
                total = total + offset * lax.rsqrt(near)
        pulls.append(total)
    return jnp.concatenate(pulls, axis=1)


def score_kernel(
    ensemble, rounded, others, incidence, base, weight, w_dec, grad_out, vertex_out, grads, both, vertices, sems
):
    members, channels, _ = base.shape
    nodes = incidence.shape[0]
    lanes = grads.shape[1]
    factor = weight[...] * (1.0 / (ensemble * (ensemble - 1)))
    copies = []
    pull = [part for m in range(members) for part in parts_of(pull_sums(rounded, others, m, members), 2)]
    at_points = at_grid(pull, incidence)
    for member in range(members):
        high, low = at_points[2 * member : 2 * member + 2]
        grad = (base[member] - factor * (low + high)).astype(BF)
        grads[member] = jnp.concatenate([grad, jnp.zeros((lanes - channels, grad.shape[1]), BF)], axis=0)
    both[...] = jnp.stack([grads[member, :channels] for member in range(members)], axis=1)
    copies.append(pltpu.make_async_copy(both, grad_out, sems.at[members]))
    copies[-1].start()
    by_node = dot_nt(incidence[...], jnp.concatenate([grads[member] for member in range(members)], axis=0))
    filled = jnp.concatenate([w_dec[...], jnp.zeros((lanes - channels, w_dec.shape[1]), BF)], axis=0)
    weights = jnp.concatenate([filled, filled], axis=0)
    for member in range(members):
        parts = parts_of(by_node[:, member * lanes : (member + 1) * lanes], 2)
        vertices[member] = dot(jnp.concatenate(parts, axis=1), weights).astype(BF)
        copies.append(pltpu.make_async_copy(vertices.at[member], vertex_out.at[member], sems.at[member]))
        copies[-1].start()
    for copy in copies:
        copy.wait()


def call(kernel, outs, ins, scratch=(), out_spec=VMEM, weight=0):
    return pl.pallas_call(
        kernel,
        out_shape=[jax.ShapeDtypeStruct(shape, kind) for shape, kind in outs],
        in_specs=ins,
        out_specs=[out_spec] * len(outs),
        scratch_shapes=[pltpu.VMEM(*spec) if isinstance(spec, tuple) else spec for spec in scratch],
        compiler_params=PARAMS,
        cost_estimate=pl.CostEstimate(flops=weight, bytes_accessed=0, transcendentals=0) if weight else None,
    )


def per_device(
    latent, noise_draw, mesh_links, w_cond, w_in, w_out, dec_gain, w_dec,
    target_vertex_map, prior_field, target, location_loss_factor,
):
    members, rows, depth = latent.shape
    channels, points = prior_field.shape
    shards = lax.axis_size("node")
    groups = lax.axis_size("member")
    ensemble = members * groups
    halo = 2 * WIN
    wide = padded(rows + halo)
    sent = (members * halo + 16, depth)
    near_pairs = [(i, i ^ 1) for i in range(shards)]
    far_pairs = [(i, (i + 1) % shards if i % 2 else (i - 1) % shards) for i in range(shards)]

    dma = pltpu.SemaphoreType.DMA

    in_hbm = functools.partial(pltpu.with_memory_space_constraint, memory_space=pltpu.HBM)

    vertex = target_vertex_map.reshape(1, points)
    near, far = call(
        functools.partial(pack_kernel, shards), [(sent, BF)] * 2, [HBM, HBM], [(mesh_links.shape, jnp.int32), dma((1 + 2 * members,))]
    )(in_hbm(latent), in_hbm(mesh_links))
    far = lax.ppermute(far, "node", far_pairs)
    near = lax.ppermute(near, "node", near_pairs)
    state, normed_own, normed_next, counts_own, scaling, incidence = call(
        functools.partial(near_kernel, shards),
        [
            ((members, rows, depth), F32),
            ((members, rows, depth), BF),
            ((members, rows, depth), BF),
            ((rows, wide), BF),
            ((w_cond.shape[0], members, depth), F32),
            ((rows, points), BF),
        ],
        [VMEM] + [HBM] * 7,
        [
            ((members, wide, depth), BF),
            ((members, rows + halo, depth), BF),
            (mesh_links.shape, jnp.int32),
            (noise_draw.shape, F32),
            (w_cond.shape, F32),
            (latent.shape, BF),
            ((1, points), jnp.int32),
            (w_in.shape[1:], BF),
            (w_out.shape[1:], BF),
            dma((7,)),
        ],
    )(near, *map(in_hbm, (mesh_links, noise_draw, w_cond, latent, vertex, w_in, w_out)))
    decoded, rounded = call(
        functools.partial(far_kernel, shards),
        [((channels, members * rows), F32), ((channels, members * rows), BF)],
        [VMEM] * 12,
        [
            ((members, 2 * halo, depth), BF),
            ((members, halo, depth), BF),
            ((members, rows + halo, depth), F32),
            ((members, wide, depth), BF),
        ],
    )(
        latent, mesh_links, far, scaling, w_in, w_out, dec_gain.reshape(1, depth), w_dec,
        state, normed_own, normed_next, counts_own,
    )
    partner = lax.ppermute(rounded, "member", [(i, i ^ 1) for i in range(groups)])
    weight = location_loss_factor.reshape(1, points)
    (base,) = call(
        functools.partial(grid_kernel, ensemble), [((members, channels, points), F32)], [VMEM] * 5
    )(decoded, prior_field, target, weight, incidence)
    partner, base = lax.optimization_barrier((partner, base))
    sides = 2
    (stacked,) = call(
        stack_kernel, [((groups // sides, channels, sides * members * rows), BF)], [VMEM] * 2
    )(rounded, partner)
    others = lax.all_to_all(
        stacked, "member", split_axis=0, concat_axis=0, tiled=True,
        axis_index_groups=[list(range(side, groups, sides)) for side in range(sides)],
    )
    grads, vertices = call(
        functools.partial(score_kernel, ensemble),
        [((channels, members, points), BF), ((members, rows, depth), BF)],
        [VMEM] * 6,
        [
            ((members, channels + -channels % 128, points), BF),
            ((channels, members, points), BF),
            ((members, rows, depth), BF),
            dma((members + 1,)),
        ],
        HBM,
    )(rounded, others, incidence, base, weight, w_dec)
    return jnp.transpose(grads, (1, 0, 2)), vertices


def solution(mesh):
    in_specs = (
        P("member", "node", None),
        P("member", None),
        P(None, "node"),
        P(),
        P(),
        P(),
        P(),
        P(),
        P("node"),
        P(None, "node"),
        P(None, "node"),
        P("node"),
    )
    out_specs = (P("member", None, "node"), P("member", "node", None))
    return jax.shard_map(
        per_device, mesh=mesh, in_specs=in_specs, out_specs=out_specs, check_vma=False
    )
```
